256 devices in a mesh: band: 32 (over y_hi, z, core), member: 8 (over y_lo, x).
Axes of the slice: x: 4, y: 4 (y_hi: 2, y_lo: 2; y = y_hi * 2 + y_lo), z: 8, core: 2. Of those that a mesh axis runs over, the one named last changes fastest.
Arguments:
- grid_latent: bfloat16 [8, 32768, 512], P('member', 'band'), may hold values from -6 to 6
- mesh_latent: bfloat16 [8, 32768, 512], P('member', 'band'), may hold values from -6 to 6
- edge_attr: bfloat16 [4, 4, 32768], P(None, None, 'band'), may hold values from -5 to 5
- neighbours: int32 [32768, 4], P('band'), may hold values from 0 to 2047, as said below
- send_rows: int32 [64, 512], P('band'), may hold values from 0 to 1023, as said below
- target: float32 [100, 32768], P(None, 'band'), may hold values from -6 to 6
- field_weight: float32 [100], replicated, may hold values from 1 to 10
- w_src: bfloat16 [512, 512], replicated, may hold values from -0.25 to 0.25
- w_dst: bfloat16 [512, 512], replicated, may hold values from -0.25 to 0.25
- w_edge: bfloat16 [4, 512], replicated, may hold values from -3 to 3
- w_msg: bfloat16 [512, 512], replicated, may hold values from -0.25 to 0.25
- ln_gain: float32 [512], replicated, may hold values from 0.1 to 1.9
- w_out: bfloat16 [512, 100], replicated, may hold values from -0.25 to 0.25
Outputs:
- d_grid: bfloat16 [8, 32768, 512], P('member', 'band')
- d_mesh: bfloat16 [8, 32768, 512], P('member', 'band')
The draws below stay inside these ranges and needn't reach their ends.
Inputs may be any that keep to these rules, and one draw needn't show every extreme that they name: `neighbours`: grid points of band index 0 never name slots 1024 to 1535, those of the last band index never name slots 1024 + 512 and up. `send_rows`: the two lists of one band index hold 1024 distinct rows together.
All inputs are finite; a program needn't handle non-finite values.
Results may differ from the reference program's by a relative error of at most 0.04.
Values may be sent and summed in bfloat16 or wider, within the bound.
A program may use at most 128 MiB of HBM per device.

```python
import math
import jax
import jax.numpy as jnp
from jax import lax

LATENT = 512
FIELDS = 100
EDGES = 4
EDGE_FEATS = 4
GRID_DEV = 1024
MESH_DEV = 1024
HALO = 512
SLOTS = 2048
MEMBERS = 8
GRID = 32768
MESH = 32768
SENDS = 64
N_BAND = 32


def draw_send_rows(key, part):
    key = jax.random.fold_in(key, 11)
    bands = SENDS // 2

    def one_band(index):
        shuffled = jax.random.permutation(jax.random.fold_in(key, index), MESH_DEV)
        return shuffled[:2 * HALO].reshape(2, HALO)
    lists = jax.vmap(one_band)(jnp.arange(bands, dtype=jnp.int32))
    return lists.reshape(SENDS, HALO).astype(jnp.int32)


def draw_neighbours(key, part):
    key = jax.random.fold_in(key, 17)
    bands = GRID // GRID_DEV
    key_kind, key_local, key_rim = jax.random.split(key, 3)
    kind = jax.random.randint(key_kind, (GRID, EDGES), 0, 4)
    local = jax.random.randint(key_local, (GRID, EDGES), 0, MESH_DEV)
    rim = jax.random.randint(key_rim, (GRID, EDGES), 0, HALO)
    device = (jnp.arange(GRID, dtype=jnp.int32) // GRID_DEV)[:, None]
    below = (kind == 2) & (device > 0)
    above = (kind == 3) & (device < bands - 1)
    slots = jnp.where(below, MESH_DEV + rim, jnp.where(above, MESH_DEV + HALO + rim, local))
    return slots.astype(jnp.int32)


def shard_levels(stream_key, shape, cuts, low, high):
    def one(dim, parts):
        steps = jax.random.uniform(jax.random.fold_in(jax.random.fold_in(stream_key, 6), dim), (parts,), jnp.float32, low / len(cuts), high / len(cuts))
        return jnp.repeat(jnp.exp(steps), shape[dim] // parts).reshape((-1,) + (1,) * (len(shape) - dim - 1))

    loudness = one(*cuts[0])
    for cut in cuts[1:]:
        loudness = loudness * one(*cut)
    return loudness


def noise(own_key, dims, deviation, reach, shards=(), held_as=jnp.bfloat16):
    values = deviation * jax.random.normal(own_key, dims, jnp.float32)
    if shards:
        values = values * shard_levels(own_key, dims, shards, -0.22, 0.18)
    return jnp.clip(values, -reach, reach).astype(held_as)


def setup_inputs(seed: int = 0) -> dict:
    key_of = jax.random.split(jax.random.key(seed), 14)
    grid_latent = noise(key_of[0], (MEMBERS, GRID, LATENT), 1.0, 6.0, ((0, 8), (1, 32)))
    mesh_latent = noise(key_of[1], (MEMBERS, MESH, LATENT), 1.0, 6.0, ((0, 8), (1, 32)))
    edge_attr = noise(key_of[2], (EDGE_FEATS, EDGES, GRID), 1.0, 5.0, ((2, 32),))
    neighbours = draw_neighbours(jax.random.fold_in(key_of[13], 71), 0)
    send_rows = draw_send_rows(jax.random.fold_in(key_of[13], 71), 0)
    target = noise(key_of[5], (FIELDS, GRID), 1.0, 6.0, ((1, 32),), jnp.float32)
    field_weight = jnp.clip(jnp.exp(jax.random.uniform(key_of[6], (FIELDS,), jnp.float32, math.log(1.0), math.log(10.0))), 1.0, 10.0)
    w_src = noise(key_of[7], (LATENT, LATENT), LATENT ** -0.5, 0.25)
    w_dst = noise(key_of[8], (LATENT, LATENT), LATENT ** -0.5, 0.25)
    w_edge = noise(key_of[9], (EDGE_FEATS, LATENT), EDGE_FEATS ** -0.5, 3.0)
    w_msg = noise(key_of[10], (LATENT, LATENT), LATENT ** -0.5, 0.25)
    ln_gain = jnp.clip(1.0 + 0.18 * jax.random.normal(key_of[11], (LATENT,), jnp.float32), 0.1, 1.9)
    w_out = noise(key_of[12], (LATENT, FIELDS), LATENT ** -0.5, 0.25)
    return {"grid_latent": grid_latent, "mesh_latent": mesh_latent, "edge_attr": edge_attr, "neighbours": neighbours, "send_rows": send_rows, "target": target, "field_weight": field_weight, "w_src": w_src, "w_dst": w_dst, "w_edge": w_edge, "w_msg": w_msg, "ln_gain": ln_gain, "w_out": w_out}


DELTA_SQ = 0.0625
ALPHA = 0.95
LN_EPS = 1e-05

def slope(diff):
    return diff / jnp.sqrt(diff * diff + DELTA_SQ)

def as_wide(value):
    return value.astype(jnp.float32)

def times_transposed(left, weight):
    return lax.dot_general(as_wide(left), as_wide(weight), (((1,), (1,)), ((), ())), preferred_element_type=jnp.float32)

def slot_tables(neighbours, send_rows):
    sends = send_rows.reshape(N_BAND, 2, HALO)
    device = jnp.arange(N_BAND, dtype=jnp.int32)
    below = jnp.maximum(device - 1, 0)
    above = jnp.minimum(device + 1, N_BAND - 1)
    own_rows = device[:, None] * MESH_DEV + jnp.arange(MESH_DEV, dtype=jnp.int32)[None, :]
    from_below = below[:, None] * MESH_DEV + sends[below, 1]
    from_above = above[:, None] * MESH_DEV + sends[above, 0]
    table = jnp.concatenate([own_rows, from_below, from_above], axis=1).astype(jnp.int32)
    local_slots = neighbours.reshape(N_BAND, GRID_DEV * EDGES).astype(jnp.int32)
    nodes = jnp.take_along_axis(table, local_slots, axis=1).reshape(GRID, EDGES)
    return (table, local_slots, nodes)

def forward_member(grid_rows, mesh_rows, nodes, edge_embed, w_src, w_dst, w_msg, ln_gain, w_out):
    src = jnp.dot(as_wide(mesh_rows), as_wide(w_src), preferred_element_type=jnp.float32).astype(jnp.bfloat16)
    dst = jnp.dot(as_wide(grid_rows), as_wide(w_dst), preferred_element_type=jnp.float32)
    pre = src[nodes].astype(jnp.float32) + dst[:, None, :] + edge_embed
    act = jax.nn.silu(pre).astype(jnp.bfloat16)
    agg = jnp.dot(as_wide(act.reshape(GRID * EDGES, LATENT)), as_wide(w_msg), preferred_element_type=jnp.float32)
    z_rows = grid_rows.astype(jnp.float32) + agg.reshape(GRID, EDGES, LATENT).sum(axis=1)
    centre = z_rows - lax.optimization_barrier(jnp.mean(z_rows, axis=1, keepdims=True))
    rstd = 1.0 / jnp.sqrt(lax.optimization_barrier(jnp.mean(centre * centre, axis=1, keepdims=True)) + LN_EPS)
    zhat = centre * rstd
    normed = (zhat * ln_gain[None, :]).astype(jnp.bfloat16)
    pred = lax.dot_general(as_wide(w_out), as_wide(normed), (((0,), (1,)), ((), ())), preferred_element_type=jnp.float32)
    return (pred, pre, zhat, rstd)

def reference(grid_latent, mesh_latent, edge_attr, neighbours, send_rows, target, field_weight, w_src, w_dst, w_edge, w_msg, ln_gain, w_out):
    table, local_slots, nodes = slot_tables(neighbours, send_rows)
    edge_embed = jnp.einsum('ekg,eh->gkh', as_wide(edge_attr), as_wide(w_edge), preferred_element_type=jnp.float32)

    def run_forward(pair):
        return forward_member(pair[0], pair[1], nodes, edge_embed, w_src, w_dst, w_msg, ln_gain, w_out)[0]
    preds = lax.map(run_forward, (grid_latent, mesh_latent))
    coeff = ALPHA / (MEMBERS - 1) + (1.0 - ALPHA) / MEMBERS

    def member_grad(own_pred):
        spread = lax.optimization_barrier(jnp.sum(slope(own_pred[None, :, :] - preds), axis=0))
        return (field_weight[:, None] * (slope(own_pred - target) - coeff * spread)).astype(jnp.bfloat16)
    d_preds = lax.map(member_grad, preds)

    def run_backward(triple):
        grid_rows, mesh_rows, d_pred = triple
        pred, pre, zhat, rstd = forward_member(grid_rows, mesh_rows, nodes, edge_embed, w_src, w_dst, w_msg, ln_gain, w_out)
        d_u = lax.dot_general(as_wide(d_pred), as_wide(w_out), (((0,), (1,)), ((), ())), preferred_element_type=jnp.float32)
        scaled = d_u * ln_gain[None, :]
        d_z = rstd * (scaled - lax.optimization_barrier(jnp.mean(scaled, axis=1, keepdims=True)) - zhat * lax.optimization_barrier(jnp.mean(scaled * zhat, axis=1, keepdims=True)))
        d_act = times_transposed(d_z.astype(jnp.bfloat16), w_msg)
        sigma = jax.nn.sigmoid(pre)
        d_pre = (d_act[:, None, :] * (sigma * (1.0 + pre * (1.0 - sigma)))).astype(jnp.bfloat16)
        d_sum = lax.optimization_barrier(jnp.sum(d_pre.astype(jnp.float32), axis=1)).astype(jnp.bfloat16)
        d_grid = (d_z + times_transposed(d_sum, w_dst)).astype(jnp.bfloat16)
        per_device = d_pre.reshape(N_BAND, GRID_DEV * EDGES, LATENT).astype(jnp.float32)
        device = jnp.arange(N_BAND, dtype=jnp.int32)[:, None]
        slot_grad = jnp.zeros((N_BAND, SLOTS, LATENT), jnp.float32).at[device, local_slots].add(per_device)
        slot_grad = slot_grad.astype(jnp.bfloat16)
        contrib = times_transposed(slot_grad.reshape(N_BAND * SLOTS, LATENT), w_src)
        d_mesh = jnp.zeros((MESH, LATENT), jnp.float32).at[table.reshape(-1)].add(contrib)
        return (d_grid, d_mesh.astype(jnp.bfloat16))
    d_grid, d_mesh = lax.map(run_backward, (grid_latent, mesh_latent, d_preds))
    return (d_grid, d_mesh)
```

```python
import functools

import jax
import jax.numpy as jnp
from jax import lax
from jax.experimental import pallas as pl
from jax.experimental.pallas import tpu as pltpu
from jax.sharding import PartitionSpec as P

DELTA_SQ = 0.0625
ALPHA = 0.95
LN_EPS = 1e-05

BF = jnp.bfloat16
F32 = jnp.float32
LANES = 128
CHUNKS = 4
MESH_ID = pl.DeviceIdType.MESH

COL_NEIGHBOUR = 100
COL_EDGE = 104
COL_SEND = 120


def dot(left, right):
    return jnp.dot(left, right, preferred_element_type=F32)


def dot_t(left, right):
    return lax.dot_general(left, right, (((1,), (1,)), ((), ())), preferred_element_type=F32)


def slope(diff):
    return diff * lax.rsqrt(diff * diff + DELTA_SQ)


def one_hot_columns(column, width):
    rows = column.shape[0]
    return jnp.where(lax.broadcasted_iota(jnp.int32, (rows, width), 1) == column, 1.0, 0.0).astype(BF)


def one_hot_rows(row, height, first):
    width = row.shape[1]
    return jnp.where(
        lax.broadcasted_iota(jnp.int32, (height, width), 0) + first == row, 1.0, 0.0
    ).astype(BF)


def kernel(
    n_band,
    n_member,
    grid_ref,
    mesh_ref,
    edge_ref,
    near_ref,
    send_ref,
    target_ref,
    weight_ref,
    w_src_ref,
    w_dst_ref,
    w_edge_ref,
    w_msg_ref,
    gain_ref,
    w_out_ref,
    d_grid_ref,
    d_mesh_ref,
    wide,
    table,
    w_out,
    src,
    out_halo,
    halo,
    own,
    deriv,
    zhat,
    rstd,
    pred,
    peers,
    d_peers,
    d_pred,
    d_halo,
    back,
    halo_send,
    halo_recv,
    pred_send,
    pred_recv,
    d_send,
    d_recv,
    back_send,
    back_recv,
):
    points, channels = grid_ref.shape
    owned = mesh_ref.shape[0]
    edges = near_ref.shape[0]
    rim = send_ref.shape[1]
    fields = target_ref.shape[0]
    chunk = points // CHUNKS
    share = chunk // n_member
    band = lax.axis_index("band")
    me = lax.axis_index("member")
    coeff = ALPHA / (n_member - 1) + (1.0 - ALPHA) / n_member

    barrier = pltpu.get_barrier_semaphore()
    for step in range(1, n_member):
        pl.semaphore_signal(
            barrier, inc=1, device_id={"member": lax.rem(me + step, n_member)}, device_id_type=MESH_ID
        )

    @pl.when(band > 0)
    def _():
        pl.semaphore_signal(barrier, inc=1, device_id={"band": band - 1}, device_id_type=MESH_ID)

    @pl.when(band < n_band - 1)
    def _():
        pl.semaphore_signal(barrier, inc=1, device_id={"band": band + 1}, device_id_type=MESH_ID)

    wide[...] = jnp.zeros_like(wide)
    wide[0:fields, :] = target_ref[...]
    wide[COL_NEIGHBOUR : COL_NEIGHBOUR + edges, :] = near_ref[...].astype(F32)
    for feature in range(edge_ref.shape[0]):
        wide[COL_EDGE + feature * edges : COL_EDGE + (feature + 1) * edges, :] = edge_ref[feature].astype(F32)
    wide[COL_SEND : COL_SEND + 1, 0:rim] = send_ref[0:1, :].astype(F32)
    wide[COL_SEND : COL_SEND + 1, rim : 2 * rim] = send_ref[1:2, :].astype(F32)
    table[...] = wide[...].T
    w_out[...] = jnp.zeros_like(w_out)
    w_out[0:fields, :] = w_out_ref[...]
    halo[2 * rim :, :] = jnp.zeros((LANES, channels), BF)
    for feature in range(edge_ref.shape[0]):
        for edge in range(edges):
            row = 2 * rim + COL_EDGE + feature * edges + edge
            halo[row : row + 1, :] = w_edge_ref[feature : feature + 1, :]

    src[...] = dot(mesh_ref[...], w_src_ref[...]).astype(BF)
    for side in range(2):
        column = table[side * rim : (side + 1) * rim, COL_SEND : COL_SEND + 1].astype(jnp.int32)
        out_halo[side] = dot(one_hot_columns(column, owned), src[...]).astype(BF)

    links = 0
    for step in range(1, n_member):
        links += 1
    pl.semaphore_wait(
        barrier, links + jnp.where(band > 0, 1, 0) + jnp.where(band < n_band - 1, 1, 0)
    )

    down = pltpu.make_async_remote_copy(
        src_ref=out_halo.at[0],
        dst_ref=halo.at[pl.ds(rim, rim)],
        send_sem=halo_send.at[0],
        recv_sem=halo_recv.at[1],
        device_id={"band": jnp.maximum(band - 1, 0)},
        device_id_type=MESH_ID,
    )
    up = pltpu.make_async_remote_copy(
        src_ref=out_halo.at[1],
        dst_ref=halo.at[pl.ds(0, rim)],
        send_sem=halo_send.at[1],
        recv_sem=halo_recv.at[0],
        device_id={"band": jnp.minimum(band + 1, n_band - 1)},
        device_id_type=MESH_ID,
    )
    has_below = band > 0
    has_above = band < n_band - 1

    @pl.when(has_below)
    def _():
        down.start()

    @pl.when(has_above)
    def _():
        up.start()

    @pl.when(jnp.logical_not(has_below))
    def _():
        halo[0:rim, :] = jnp.zeros((rim, channels), BF)
        back[0:rim, :] = jnp.zeros((rim, channels), BF)

    @pl.when(jnp.logical_not(has_above))
    def _():
        halo[rim : 2 * rim, :] = jnp.zeros((rim, channels), BF)
        back[rim : 2 * rim, :] = jnp.zeros((rim, channels), BF)

    def gather_own(part, _):
        first = pl.multiple_of(part * chunk, chunk)
        hot = jnp.concatenate(
            [
                one_hot_columns(
                    table[pl.ds(first, chunk), COL_NEIGHBOUR + edge : COL_NEIGHBOUR + edge + 1].astype(
                        jnp.int32
                    ),
                    owned,
                )
                for edge in range(edges)
            ],
            axis=0,
        )
        rows = dot(hot, src[...]).astype(BF)
        for edge in range(edges):
            own[edge, pl.ds(first, chunk), :] = rows[edge * chunk : (edge + 1) * chunk, :]
        return 0

    lax.fori_loop(0, CHUNKS, gather_own, 0)

    @pl.when(has_above)
    def _():
        down.wait_recv()

    @pl.when(has_below)
    def _():
        up.wait_recv()

    gain = gain_ref[...]

    def forward(part):
        rows = pl.ds(part * chunk, chunk)
        lane = lax.broadcasted_iota(jnp.int32, (chunk, LANES), 1)
        features = table[rows, :]
        hots = []
        for edge in range(edges):
            column = table[rows, COL_NEIGHBOUR + edge : COL_NEIGHBOUR + edge + 1].astype(jnp.int32)
            chosen = (lane >= COL_EDGE) & (lane < COL_SEND) & (lax.rem(lane, edges) == edge)
            hots.append(
                jnp.concatenate(
                    [
                        one_hot_columns(column - owned, 2 * rim),
                        jnp.where(chosen, features, 0.0).astype(BF),
                    ],
                    axis=1,
                )
            )
        read = dot(jnp.concatenate(hots, axis=0), halo[...])
        dst = dot(grid_ref[rows, :], w_dst_ref[...])
        total = None
        for edge in range(edges):
            pre = read[edge * chunk : (edge + 1) * chunk, :] + own[edge, rows, :].astype(F32) + dst
            sigma = 0.5 * jnp.tanh(0.5 * pre) + 0.5
            act = pre * sigma
            deriv[edge, rows, :] = (sigma + act * (1.0 - sigma)).astype(BF)
            total = act if total is None else total + act
        z = grid_ref[rows, :].astype(F32) + dot(total.astype(BF), w_msg_ref[...])
        centre = z - jnp.mean(z, axis=1, keepdims=True)
        scale = lax.rsqrt(jnp.mean(centre * centre, axis=1, keepdims=True) + LN_EPS)
        hat = centre * scale
        zhat[rows, :] = hat
        rstd[rows, :] = jnp.broadcast_to(scale, (chunk, LANES))
        pred[rows, :] = dot_t((hat * gain).astype(BF), w_out[...]).astype(BF)

    def pred_copy(part, other):
        return pltpu.make_async_remote_copy(
            src_ref=pred.at[pl.ds(part * chunk + other * share, share)],
            dst_ref=peers.at[me, pl.ds(part * share, share)],
            send_sem=pred_send.at[part, other],
            recv_sem=pred_recv.at[part, me],
            device_id={"member": other},
            device_id_type=MESH_ID,
        )

    def pred_arrival(part, other):
        return pltpu.make_async_remote_copy(
            src_ref=pred.at[pl.ds(part * chunk + other * share, share)],
            dst_ref=peers.at[other, pl.ds(part * share, share)],
            send_sem=pred_send.at[part, other],
            recv_sem=pred_recv.at[part, other],
            device_id={"member": other},
            device_id_type=MESH_ID,
        )

    def grad_copy(part, other):
        return pltpu.make_async_remote_copy(
            src_ref=d_peers.at[other, pl.ds(part * share, share)],
            dst_ref=d_pred.at[pl.ds(part * chunk + me * share, share)],
            send_sem=d_send.at[part, other],
            recv_sem=d_recv.at[part, me],
            device_id={"member": other},
            device_id_type=MESH_ID,
        )

    def grad_arrival(part, other):
        return pltpu.make_async_remote_copy(
            src_ref=d_peers.at[other, pl.ds(part * share, share)],
            dst_ref=d_pred.at[pl.ds(part * chunk + other * share, share)],
            send_sem=d_send.at[part, other],
            recv_sem=d_recv.at[part, other],
            device_id={"member": other},
            device_id_type=MESH_ID,
        )

    def others():
        return [lax.rem(me + step, n_member) for step in range(1, n_member)]

    def send_pred(part):
        for other in others():
            pred_copy(part, other).start()
        mine = pl.multiple_of(part * chunk + me * share, share)
        peers[me, part * share : (part + 1) * share, :] = pred[pl.ds(mine, share), :]

    def compare(part):
        for other in others():
            pred_arrival(part, other).wait_recv()
        rows = slice(part * share, (part + 1) * share)
        mine = pl.multiple_of(part * chunk + me * share, share)
        goal = table[pl.ds(mine, share), :]
        lane = lax.broadcasted_iota(jnp.int32, (share, LANES), 1)
        goal = jnp.where(lane < fields, goal, 0.0)
        values = [peers[member, rows, :].astype(F32) for member in range(n_member)]
        spread = [jnp.zeros((share, LANES), F32) for _ in range(n_member)]
        for left in range(n_member):
            for right in range(left + 1, n_member):
                step = slope(values[left] - values[right])
                spread[left] = spread[left] + step
                spread[right] = spread[right] - step
        for member in range(n_member):
            grad = weight_ref[...] * (slope(values[member] - goal) - coeff * spread[member])
            d_peers[member, rows, :] = grad.astype(BF)
        for other in others():
            grad_copy(part, other).start()
        d_pred[pl.ds(mine, share), :] = d_peers[me, rows, :]

    def backward(part):
        for other in others():
            grad_arrival(part, other).wait_recv()
        rows = pl.ds(part * chunk, chunk)
        hat = zhat[rows, :]
        scale = rstd[rows, 0:1]
        scaled = dot(d_pred[rows, :], w_out[...]) * gain
        d_z = scale * (
            scaled
            - jnp.mean(scaled, axis=1, keepdims=True)
            - hat * jnp.mean(scaled * hat, axis=1, keepdims=True)
        )
        d_act = dot_t(d_z.astype(BF), w_msg_ref[...])
        total = None
        for edge in range(edges):
            d_pre = (d_act * deriv[edge, rows, :].astype(F32)).astype(BF)
            deriv[edge, rows, :] = d_pre
            total = d_pre.astype(F32) if total is None else total + d_pre.astype(F32)
        d_grid_ref[rows, :] = (d_z + dot_t(total.astype(BF), w_dst_ref[...])).astype(BF)

    forward(0)
    send_pred(0)
    forward(1)
    send_pred(1)
    compare(0)
    forward(2)
    send_pred(2)
    compare(1)
    forward(3)
    send_pred(3)
    compare(2)
    backward(0)
    compare(3)
    backward(1)
    backward(2)
    backward(3)

    def scatter(first, height):
        total = None
        for edge in range(edges):
            part = dot(one_hot_rows(near_ref[edge : edge + 1, :], height, first), deriv[edge])
            total = part if total is None else total + part
        return total

    to_below = pltpu.make_async_remote_copy(
        src_ref=d_halo.at[0],
        dst_ref=back.at[pl.ds(rim, rim)],
        send_sem=back_send.at[0],
        recv_sem=back_recv.at[1],
        device_id={"band": jnp.maximum(band - 1, 0)},
        device_id_type=MESH_ID,
    )
    to_above = pltpu.make_async_remote_copy(
        src_ref=d_halo.at[1],
        dst_ref=back.at[pl.ds(0, rim)],
        send_sem=back_send.at[1],
        recv_sem=back_recv.at[0],
        device_id={"band": jnp.minimum(band + 1, n_band - 1)},
        device_id_type=MESH_ID,
    )
    d_halo[0] = scatter(owned, rim).astype(BF)

    @pl.when(has_below)
    def _():
        to_below.start()

    d_halo[1] = scatter(owned + rim, rim).astype(BF)

    @pl.when(has_above)
    def _():
        to_above.start()

    total = scatter(0, owned)

    @pl.when(has_above)
    def _():
        to_below.wait_recv()

    @pl.when(has_below)
    def _():
        to_above.wait_recv()

    for side in range(2):
        total = total + dot(
            one_hot_rows(send_ref[side : side + 1, :], owned, 0), back[side * rim : (side + 1) * rim, :]
        )
    d_mesh_ref[...] = dot_t(total.astype(BF), w_src_ref[...]).astype(BF)

    @pl.when(has_below)
    def _():
        down.wait_send()
        to_below.wait_send()

    @pl.when(has_above)
    def _():
        up.wait_send()
        to_above.wait_send()

    for part in range(CHUNKS):
        for other in others():
            pred_copy(part, other).wait_send()
            grad_copy(part, other).wait_send()


def per_device(
    n_band,
    n_member,
    grid_latent,
    mesh_latent,
    edge_attr,
    neighbours,
    send_rows,
    target,
    field_weight,
    w_src,
    w_dst,
    w_edge,
    w_msg,
    ln_gain,
    w_out,
):
    grid_rows = grid_latent[0]
    mesh_rows = mesh_latent[0]
    points, channels = grid_rows.shape
    owned = mesh_rows.shape[0]
    edges = neighbours.shape[1]
    rim = send_rows.shape[1]
    fields = target.shape[0]
    share = points // n_member
    weights = jnp.pad(field_weight, (0, LANES - fields)).reshape(1, LANES)
    vmem = pl.BlockSpec(memory_space=pltpu.VMEM)
    dma = pltpu.SemaphoreType.DMA
    d_grid, d_mesh = pl.pallas_call(
        functools.partial(kernel, n_band, n_member),
        out_shape=(
            jax.ShapeDtypeStruct((points, channels), BF),
            jax.ShapeDtypeStruct((owned, channels), BF),
        ),
        in_specs=[vmem] * 13,
        out_specs=(vmem, vmem),
        scratch_shapes=[
            pltpu.VMEM((LANES, points), F32),
            pltpu.VMEM((points, LANES), F32),
            pltpu.VMEM((LANES, channels), BF),
            pltpu.VMEM((owned, channels), BF),
            pltpu.VMEM((2, rim, channels), BF),
            pltpu.VMEM((2 * rim + LANES, channels), BF),
            pltpu.VMEM((edges, points, channels), BF),
            pltpu.VMEM((edges, points, channels), BF),
            pltpu.VMEM((points, channels), F32),
            pltpu.VMEM((points, LANES), F32),
            pltpu.VMEM((points, LANES), BF),
            pltpu.VMEM((n_member, share, LANES), BF),
            pltpu.VMEM((n_member, share, LANES), BF),
            pltpu.VMEM((points, LANES), BF),
            pltpu.VMEM((2, rim, channels), BF),
            pltpu.VMEM((2 * rim, channels), BF),
            dma((2,)),
            dma((2,)),
            dma((CHUNKS, n_member)),
            dma((CHUNKS, n_member)),
            dma((CHUNKS, n_member)),
            dma((CHUNKS, n_member)),
            dma((2,)),
            dma((2,)),
        ],
        compiler_params=pltpu.CompilerParams(
            collective_id=0, has_side_effects=True, vmem_limit_bytes=58 * 2**20
        ),
    )(
        grid_rows,
        mesh_rows,
        edge_attr,
        neighbours.T,
        send_rows,
        target,
        weights,
        w_src,
        w_dst,
        w_edge,
        w_msg,
        ln_gain.reshape(1, channels),
        w_out.T,
    )
    return d_grid[None], d_mesh[None]


def solution(mesh):
    placed = (
        P("member", "band", None),
        P("member", "band", None),
        P(None, None, "band"),
        P("band", None),
        P("band", None),
        P(None, "band"),
        P(),
        P(),
        P(),
        P(),
        P(),
        P(),
        P(),
    )
    return jax.shard_map(
        functools.partial(per_device, mesh.shape["band"], mesh.shape["member"]),
        mesh=mesh,
        in_specs=placed,
        out_specs=(P("member", "band", None), P("member", "band", None)),
        check_vma=False,
    )
```

```python
import functools

import jax
import jax.numpy as jnp
from jax import lax
from jax.experimental import pallas as pl
from jax.experimental.pallas import tpu as pltpu
from jax.sharding import PartitionSpec as P

DELTA_SQ = 0.0625
ALPHA = 0.95
LN_EPS = 1e-05

BF = jnp.bfloat16
F32 = jnp.float32
LANES = 128
CHUNKS = 4
MESH_ID = pl.DeviceIdType.MESH

COL_KNOWN = 100
COL_EDGE = 104
COL_FAR = 120


def dot(left, right):
    return jnp.dot(left, right, preferred_element_type=F32)


def dot_t(left, right):
    return lax.dot_general(left, right, (((1,), (1,)), ((), ())), preferred_element_type=F32)


def slope(diff):
    return diff * lax.rsqrt(diff * diff + DELTA_SQ)


def one_hot_columns(column, width):
    rows = column.shape[0]
    return jnp.where(lax.broadcasted_iota(jnp.int32, (rows, width), 1) == column, 1.0, 0.0).astype(BF)


def one_hot_rows(row, height, first):
    width = row.shape[1]
    return jnp.where(
        lax.broadcasted_iota(jnp.int32, (height, width), 0) + first == row, 1.0, 0.0
    ).astype(BF)


def remote(src, dst, send_sem, recv_sem, **where):
    return pltpu.make_async_remote_copy(
        src_ref=src, dst_ref=dst, send_sem=send_sem, recv_sem=recv_sem, device_id=where, device_id_type=MESH_ID
    )


def kernel(n_band, n_member, *refs):
    hbm, (d_grid_hbm, total_hbm), refs = refs[:13], refs[13:15], refs[15:]
    held, refs = refs[:13], refs[13:]
    (
        grid_ref,
        mesh_ref,
        edge_ref,
        near_ref,
        send_ref,
        target_ref,
        weight_ref,
        w_src_ref,
        w_dst_ref,
        w_edge_ref,
        w_msg_ref,
        gain_ref,
        w_out_ref,
    ) = held
    (
        lists,
        wide,
        table,
        w_out,
        weights,
        columns,
        known,
        out_halo,
        away,
        base,
        read_even,
        read_odd,
        deriv,
        deriv_sum,
        zhat,
        rstd,
        pred,
        peers,
        d_peers,
        d_pred,
        d_sum,
        d_grid,
        slots,
        rims,
        d_halo,
        back,
        sums,
        load_sem,
        store_sem,
        halo_send,
        halo_recv,
        pred_send,
        pred_recv,
        d_send,
        d_recv,
        back_send,
        back_recv,
    ) = refs
    points, channels = grid_ref.shape
    owned = mesh_ref.shape[0]
    features = edge_ref.shape[0]
    edges = near_ref.shape[0]
    rim = send_ref.shape[1]
    fields = target_ref.shape[0]
    chunk = points // CHUNKS
    share = chunk // n_member
    band = lax.axis_index("band")
    me = lax.axis_index("member")
    has_below = band > 0
    has_above = band < n_band - 1
    far = lax.rem(band, 2)
    near = 1 - far
    has_far = ((far == 0) & has_below) | ((far == 1) & has_above)
    near_band = band + 2 * near - 1
    far_band = jnp.clip(band + 2 * far - 1, 0, n_band - 1)
    coeff = ALPHA / (n_member - 1) + (1.0 - ALPHA) / n_member

    def others():
        return [lax.rem(me + step, n_member) for step in range(1, n_member)]

    barrier = pltpu.get_barrier_semaphore()

    @pl.when(has_below)
    def _():
        pl.semaphore_signal(barrier, inc=1, device_id={"band": band - 1}, device_id_type=MESH_ID)

    @pl.when(has_above)
    def _():
        pl.semaphore_signal(barrier, inc=1, device_id={"band": band + 1}, device_id_type=MESH_ID)

    for other in others():
        pl.semaphore_signal(barrier, inc=1, device_id={"member": other}, device_id_type=MESH_ID)

    loads = [pltpu.make_async_copy(hbm[i], held[i], load_sem.at[i]) for i in range(13)]
    for i in (4, 1, 7, 3, 0, 8, 2, 5, 9, 10, 11, 12, 6):
        loads[i].start()

    loads[4].wait()
    lists[...] = jnp.zeros_like(lists)
    lists[0:1, 0:rim] = send_ref[0:1, :].astype(F32)
    lists[0:1, rim : 2 * rim] = send_ref[1:2, :].astype(F32)
    columns[...] = lists[...].T
    loads[1].wait()
    loads[7].wait()
    known[0:owned, :] = (0.5 * dot(mesh_ref[...], w_src_ref[...])).astype(BF)

    def select(side):
        rows = pl.ds(pl.multiple_of(side * rim, rim), rim)
        hot = one_hot_columns(columns[rows, 0:1].astype(jnp.int32), owned)
        return dot(hot, known[0:owned, :]).astype(BF)

    to_near = remote(
        out_halo.at[0], known.at[pl.ds(owned, rim)], halo_send.at[0], halo_recv.at[0], band=near_band
    )
    to_far = remote(out_halo.at[1], away.at[pl.ds(0, rim)], halo_send.at[1], halo_recv.at[1], band=far_band)
    out_halo[1] = select(far)
    pl.semaphore_wait(
        barrier, n_member - 1 + jnp.where(has_below, 1, 0) + jnp.where(has_above, 1, 0)
    )

    @pl.when(has_far)
    def _():
        to_far.start()

    out_halo[0] = select(near)
    to_near.start()

    @pl.when(jnp.logical_not(has_far))
    def _():
        away[0:rim, :] = jnp.zeros((rim, channels), BF)
        back[rim : 2 * rim, :] = jnp.zeros((rim, channels), BF)

    for i in (3, 2, 5, 9, 12, 6, 11):
        loads[i].wait()
    names = near_ref[...]
    in_near = (names >= owned + near * rim) & (names < owned + (near + 1) * rim)
    known_names = jnp.where(in_near, names - near * rim, jnp.where(names < owned, names, -1))
    wide[...] = jnp.zeros_like(wide)
    wide[0:fields, :] = target_ref[...]
    wide[COL_KNOWN : COL_KNOWN + edges, :] = known_names.astype(F32)
    wide[COL_FAR : COL_FAR + edges, :] = (names - owned - far * rim).astype(F32)
    for feature in range(features):
        wide[COL_EDGE + feature * edges : COL_EDGE + (feature + 1) * edges, :] = edge_ref[feature].astype(F32)
    table[...] = wide[...].T
    w_out[...] = jnp.zeros_like(w_out)
    w_out[0:fields, :] = w_out_ref[...]
    weights[...] = jnp.zeros_like(weights)
    weights[0:1, 0:fields] = weight_ref[...]
    away[rim:, :] = jnp.zeros((LANES, channels), BF)
    for feature in range(features):
        half = (0.5 * w_edge_ref[feature : feature + 1, :].astype(F32)).astype(BF)
        for edge in range(edges):
            row = rim + COL_EDGE + feature * edges + edge
            away[row : row + 1, :] = half
    loads[0].wait()
    loads[8].wait()
    zhat[...] = 0.5 * dot(grid_ref[...], w_dst_ref[...])
    to_near.wait_recv()

    def gather_known(part, _):
        rows = pl.ds(pl.multiple_of(part * chunk, chunk), chunk)
        hot = jnp.concatenate(
            [
                one_hot_columns(
                    table[rows, COL_KNOWN + edge : COL_KNOWN + edge + 1].astype(jnp.int32), owned + rim
                )
                for edge in range(edges)
            ],
            axis=0,
        )
        found = dot(hot, known[...])
        dst = zhat[rows, :]
        for edge in range(edges):
            base[edge, rows, :] = found[edge * chunk : (edge + 1) * chunk, :] + dst
        return 0

    lax.fori_loop(0, CHUNKS, gather_known, 0)
    loads[10].wait()

    @pl.when(has_far)
    def _():
        to_far.wait_recv()

    gain = gain_ref[...]
    reads = (read_even, read_odd)

    def read(part):
        rows = pl.ds(part * chunk, chunk)
        lane = lax.broadcasted_iota(jnp.int32, (chunk, LANES), 1)
        values = table[rows, :]
        hots = []
        for edge in range(edges):
            column = table[rows, COL_FAR + edge : COL_FAR + edge + 1].astype(jnp.int32)
            chosen = (lane >= COL_EDGE) & (lane < COL_FAR) & (lax.rem(lane, edges) == edge)
            hots.append(
                jnp.concatenate(
                    [
                        one_hot_columns(column, rim),
                        jnp.where(chosen, values, 0.0).astype(BF),
                    ],
                    axis=1,
                )
            )
        reads[part % 2][...] = dot(jnp.concatenate(hots, axis=0), away[...])

    def forward(part):
        rows = pl.ds(part * chunk, chunk)
        total = None
        derivs = None
        for edge in range(edges):
            half = reads[part % 2][edge * chunk : (edge + 1) * chunk, :] + base[edge, rows, :]
            rise = jnp.tanh(half) + 1.0
            act = half * rise
            twice = rise + act * (2.0 - rise)
            deriv[edge, rows, :] = twice.astype(BF)
            total = act if total is None else total + act
            derivs = twice if derivs is None else derivs + twice
        deriv_sum[rows, :] = derivs
        z = grid_ref[rows, :].astype(F32) + dot(total.astype(BF), w_msg_ref[...])
        centre = z - jnp.mean(z, axis=1, keepdims=True)
        scale = lax.rsqrt(jnp.mean(centre * centre, axis=1, keepdims=True) + LN_EPS)
        hat = centre * scale
        zhat[rows, :] = hat
        rstd[rows, :] = jnp.broadcast_to(scale, (chunk, LANES))
        pred[rows, :] = dot_t((hat * gain).astype(BF), w_out[...]).astype(BF)

    def pred_copy(part, other):
        return remote(
            pred.at[pl.ds(part * chunk + other * share, share)],
            peers.at[me, pl.ds(part * share, share)],
            pred_send,
            pred_recv.at[part],
            member=other,
        )

    def grad_copy(part, other):
        return remote(
            d_peers.at[other, pl.ds(part * share, share)],
            d_pred.at[pl.ds(part * chunk + me * share, share)],
            d_send,
            d_recv.at[part],
            member=other,
        )

    def all_of(count, send_sem, recv_sem):
        size = pl.ds(0, count * share)
        return remote(pred.at[size], d_pred.at[size], send_sem, recv_sem, member=lax.rem(me + 1, n_member))

    def send_pred(part):
        for other in others():
            pred_copy(part, other).start()
        mine = pl.multiple_of(part * chunk + me * share, share)
        peers[me, part * share : (part + 1) * share, :] = pred[pl.ds(mine, share), :]

    def compare(part):
        all_of(n_member - 1, pred_send, pred_recv.at[part]).wait_recv()
        rows = slice(part * share, (part + 1) * share)
        mine = pl.multiple_of(part * chunk + me * share, share)
        goal = table[pl.ds(mine, share), :]
        lane = lax.broadcasted_iota(jnp.int32, (share, LANES), 1)
        goal = jnp.where(lane < fields, goal, 0.0)
        values = [peers[member, rows, :].astype(F32) for member in range(n_member)]
        spread = [jnp.zeros((share, LANES), F32) for _ in range(n_member)]
        for left in range(n_member):
            for right in range(left + 1, n_member):
                step = slope(values[left] - values[right])
                spread[left] = spread[left] + step
                spread[right] = spread[right] - step
        for member in range(n_member):
            grad = weights[...] * (slope(values[member] - goal) - coeff * spread[member])
            d_peers[member, rows, :] = grad.astype(BF)
        for other in others():
            grad_copy(part, other).start()
        d_pred[pl.ds(mine, share), :] = d_peers[me, rows, :]

    def backward(part):
        all_of(n_member - 1, d_send, d_recv.at[part]).wait_recv()
        rows = pl.ds(part * chunk, chunk)
        hat = zhat[rows, :]
        scale = rstd[rows, 0:1]
        scaled = dot(d_pred[rows, :], w_out[...]) * gain
        d_z = scale * (
            scaled
            - jnp.mean(scaled, axis=1, keepdims=True)
            - hat * jnp.mean(scaled * hat, axis=1, keepdims=True)
        )
        zhat[rows, :] = d_z
        d_act = 0.5 * dot_t(d_z.astype(BF), w_msg_ref[...])
        d_sum[rows, :] = (d_act * deriv_sum[rows, :]).astype(BF)
        d_act = d_act.astype(BF)
        for edge in range(edges):
            deriv[edge, rows, :] = d_act * deriv[edge, rows, :]

    def scatter(part, parts, first, height):
        size = points // parts
        rows = pl.ds(part * size, size)
        names = jnp.concatenate([near_ref[edge : edge + 1, rows] for edge in range(edges)], axis=1)
        grads = jnp.concatenate([deriv[edge, rows, :] for edge in range(edges)], axis=0)
        return dot(one_hot_rows(names, height, first), grads)

    def scatter_far(part):
        found = scatter(part, CHUNKS, owned + far * rim, rim)
        if part == 0:
            rims[...] = found
        elif part < CHUNKS - 1:
            rims[...] += found
        else:
            d_halo[1] = (rims[...] + found).astype(BF)

    read(0)
    read(1)
    forward(0)
    send_pred(0)
    read(2)
    forward(1)
    send_pred(1)
    compare(0)
    read(3)
    forward(2)
    send_pred(2)
    compare(1)
    forward(3)
    send_pred(3)
    compare(2)
    backward(0)
    scatter_far(0)
    backward(1)
    scatter_far(1)
    compare(3)
    backward(2)
    scatter_far(2)
    backward(3)
    scatter_far(3)

    back_near = remote(
        d_halo.at[0], back.at[pl.ds(0, rim)], back_send.at[0], back_recv.at[0], band=near_band
    )
    back_far = remote(
        d_halo.at[1], back.at[pl.ds(rim, rim)], back_send.at[1], back_recv.at[1], band=far_band
    )

    @pl.when(has_far)
    def _():
        back_far.start()

    d_halo[0] = scatter(0, 1, owned + near * rim, rim).astype(BF)
    back_near.start()
    d_grid[...] = (zhat[...] + dot_t(d_sum[...], w_dst_ref[...])).astype(BF)
    grid_out = pltpu.make_async_copy(d_grid, d_grid_hbm, store_sem.at[0])
    grid_out.start()
    slots[...] = scatter(0, 1, 0, owned)

    def returned(side, place):
        return dot(
            one_hot_rows(send_ref[pl.ds(side, 1), :], owned, 0), back[place * rim : (place + 1) * rim, :]
        )

    back_near.wait_recv()
    slots[...] += returned(near, 0)

    @pl.when(has_far)
    def _():
        back_far.wait_recv()

    sums[...] = (slots[...] + returned(far, 1)).astype(BF)
    total_out = pltpu.make_async_copy(sums, total_hbm, store_sem.at[1])
    total_out.start()

    to_near.wait_send()
    back_near.wait_send()

    @pl.when(has_far)
    def _():
        to_far.wait_send()
        back_far.wait_send()

    all_of(CHUNKS * (n_member - 1), pred_send, pred_recv.at[0]).wait_send()
    all_of(CHUNKS * (n_member - 1), d_send, d_recv.at[0]).wait_send()
    grid_out.wait()
    total_out.wait()


def finish(grid_in, sums_hbm, w_src_hbm, grid_out, mesh_out, sums, w_src, rows_out, load_sem, store_sem):
    through = pltpu.make_async_copy(grid_in, grid_out, store_sem.at[0])
    weight = pltpu.make_async_copy(w_src_hbm, w_src, load_sem.at[0])
    values = pltpu.make_async_copy(sums_hbm, sums, load_sem.at[1])
    weight.start()
    values.start()
    through.start()
    weight.wait()
    values.wait()
    height = sums.shape[0] // 2
    stores = []
    for part in range(2):
        rows = pl.ds(part * height, height)
        rows_out[rows, :] = dot_t(sums[rows, :], w_src[...]).astype(BF)
        stores.append(
            pltpu.make_async_copy(rows_out.at[rows], mesh_out.at[rows], store_sem.at[part + 1])
        )
        stores[-1].start()
    through.wait()
    for store in stores:
        store.wait()


def per_device(
    n_band,
    n_member,
    grid_latent,
    mesh_latent,
    edge_attr,
    neighbours,
    send_rows,
    target,
    field_weight,
    w_src,
    w_dst,
    w_edge,
    w_msg,
    ln_gain,
    w_out,
):
    grid_rows = grid_latent[0]
    mesh_rows = mesh_latent[0]
    points, channels = grid_rows.shape
    owned = mesh_rows.shape[0]
    edges = neighbours.shape[1]
    rim = send_rows.shape[1]
    fields = target.shape[0]
    share = points // n_member
    chunk = points // CHUNKS
    operands = (
        grid_rows,
        mesh_rows,
        edge_attr,
        neighbours.T,
        send_rows,
        target,
        field_weight.reshape(1, fields),
        w_src,
        w_dst,
        w_edge,
        w_msg,
        ln_gain.reshape(1, channels),
        w_out.T,
    )
    anywhere = pl.BlockSpec(memory_space=pl.ANY)
    dma = pltpu.SemaphoreType.DMA
    latents = pltpu.VMEM((points, channels), BF)
    wide_latents = pltpu.VMEM((points, channels), F32)
    d_grid, sums = pl.pallas_call(
        functools.partial(kernel, n_band, n_member),
        out_shape=(
            jax.ShapeDtypeStruct((points, channels), BF),
            jax.ShapeDtypeStruct((owned, channels), BF),
        ),
        in_specs=[anywhere] * len(operands),
        out_specs=(anywhere, anywhere),
        scratch_shapes=[pltpu.VMEM(operand.shape, operand.dtype) for operand in operands]
        + [
            pltpu.VMEM((8, 2 * rim), F32),
            pltpu.VMEM((LANES, points), F32),
            pltpu.VMEM((points, LANES), F32),
            pltpu.VMEM((LANES, channels), BF),
            pltpu.VMEM((1, LANES), F32),
            pltpu.VMEM((2 * rim, 8), F32),
            pltpu.VMEM((owned + rim, channels), BF),
            pltpu.VMEM((2, rim, channels), BF),
            pltpu.VMEM((rim + LANES, channels), BF),
            pltpu.VMEM((edges, points, channels), F32),
            pltpu.VMEM((edges * chunk, channels), F32),
            pltpu.VMEM((edges * chunk, channels), F32),
            pltpu.VMEM((edges, points, channels), BF),
            wide_latents,
            wide_latents,
            pltpu.VMEM((points, LANES), F32),
            pltpu.VMEM((points, LANES), BF),
            pltpu.VMEM((n_member, share, LANES), BF),
            pltpu.VMEM((n_member, share, LANES), BF),
            pltpu.VMEM((points, LANES), BF),
            latents,
            latents,
            wide_latents,
            pltpu.VMEM((rim, channels), F32),
            pltpu.VMEM((2, rim, channels), BF),
            pltpu.VMEM((2 * rim, channels), BF),
            latents,
            dma((len(operands),)),
            dma((2,)),
            dma((2,)),
            dma((2,)),
            dma,
            dma((CHUNKS,)),
            dma,
            dma((CHUNKS,)),
            dma((2,)),
            dma((2,)),
        ],
        compiler_params=pltpu.CompilerParams(
            collective_id=0, has_side_effects=True, vmem_limit_bytes=58 * 2**20
        ),
    )(*operands)
    d_grid, d_mesh = pl.pallas_call(
        finish,
        out_shape=(
            jax.ShapeDtypeStruct((points, channels), BF),
            jax.ShapeDtypeStruct((owned, channels), BF),
        ),
        in_specs=[anywhere] * 3,
        out_specs=(anywhere, anywhere),
        scratch_shapes=[latents, pltpu.VMEM(w_src.shape, BF), latents, dma((2,)), dma((3,))],
        compiler_params=pltpu.CompilerParams(vmem_limit_bytes=16 * 2**20),
    )(d_grid, sums, w_src)
    return d_grid[None], d_mesh[None]


def solution(mesh):
    placed = (
        P("member", "band", None),
        P("member", "band", None),
        P(None, None, "band"),
        P("band", None),
        P("band", None),
        P(None, "band"),
        P(),
        P(),
        P(),
        P(),
        P(),
        P(),
        P(),
    )
    return jax.shard_map(
        functools.partial(per_device, mesh.shape["band"], mesh.shape["member"]),
        mesh=mesh,
        in_specs=placed,
        out_specs=(P("member", "band", None), P("member", "band", None)),
        check_vma=False,
    )
```

```python
import functools

import jax
import jax.numpy as jnp
from jax import lax
from jax.experimental import pallas as pl
from jax.experimental.pallas import tpu as pltpu
from jax.sharding import PartitionSpec as P

DELTA_SQ = 0.0625
ALPHA = 0.95
LN_EPS = 1e-05

BF = jnp.bfloat16
F32 = jnp.float32
LANES = 128
PARTS = (3, 3, 2)
UNIT = 128
MESH_ID = pl.DeviceIdType.MESH

COL_KNOWN = 100
COL_EDGE = 104
COL_FAR = 120


def dot(left, right):
    return jnp.dot(left, right, preferred_element_type=F32)


def dot_t(left, right):
    return lax.dot_general(left, right, (((1,), (1,)), ((), ())), preferred_element_type=F32)


def slope(diff):
    return diff * lax.rsqrt(diff * diff + DELTA_SQ)


def one_hot_columns(column, width):
    rows = column.shape[0]
    return jnp.where(lax.broadcasted_iota(jnp.int32, (rows, width), 1) == column, 1.0, 0.0).astype(BF)


def one_hot_rows(row, height, first):
    width = row.shape[1]
    return jnp.where(
        lax.broadcasted_iota(jnp.int32, (height, width), 0) + first == row, 1.0, 0.0
    ).astype(BF)


def remote(src, dst, send_sem, recv_sem, **where):
    return pltpu.make_async_remote_copy(
        src_ref=src, dst_ref=dst, send_sem=send_sem, recv_sem=recv_sem, device_id=where, device_id_type=MESH_ID
    )


def kernel(n_band, n_member, *refs):
    hbm, (d_grid, sums), refs = refs[:13], refs[13:15], refs[15:]
    held, refs = refs[:13], refs[13:]
    (
        grid_ref,
        mesh_ref,
        edge_ref,
        near_ref,
        send_ref,
        target_ref,
        weight_ref,
        w_src_ref,
        w_dst_ref,
        w_edge_ref,
        w_msg_ref,
        gain_ref,
        w_out_ref,
    ) = held
    (
        lists,
        wide,
        table,
        w_out,
        weights,
        columns,
        known,
        out_halo,
        away,
        base,
        read_even,
        read_odd,
        deriv,
        deriv_sum,
        zhat,
        rstd,
        pred,
        peers,
        d_peers,
        d_pred,
        d_sum,
        slots,
        rims,
        d_halo,
        back,
        load_sem,
        halo_send,
        halo_recv,
        pred_send,
        pred_recv,
        d_send,
        d_recv,
        back_send,
        back_recv,
    ) = refs
    points, channels = grid_ref.shape
    owned = mesh_ref.shape[0]
    features = edge_ref.shape[0]
    edges = near_ref.shape[0]
    rim = send_ref.shape[1]
    fields = target_ref.shape[0]
    firsts = [sum(PARTS[:part]) * UNIT for part in range(len(PARTS))]
    sizes = [part * UNIT for part in PARTS]
    shares = [size // n_member for size in sizes]
    owns = [first // n_member for first in firsts]
    band = lax.axis_index("band")
    me = lax.axis_index("member")
    has_below = band > 0
    has_above = band < n_band - 1
    far = lax.rem(band, 2)
    near = 1 - far
    has_far = ((far == 0) & has_below) | ((far == 1) & has_above)
    near_band = band + 2 * near - 1
    far_band = jnp.clip(band + 2 * far - 1, 0, n_band - 1)
    coeff = ALPHA / (n_member - 1) + (1.0 - ALPHA) / n_member

    def others():
        return [lax.rem(me + step, n_member) for step in range(1, n_member)]

    barrier = pltpu.get_barrier_semaphore()

    @pl.when(has_below)
    def _():
        pl.semaphore_signal(barrier, inc=1, device_id={"band": band - 1}, device_id_type=MESH_ID)

    @pl.when(has_above)
    def _():
        pl.semaphore_signal(barrier, inc=1, device_id={"band": band + 1}, device_id_type=MESH_ID)

    for other in others():
        pl.semaphore_signal(barrier, inc=1, device_id={"member": other}, device_id_type=MESH_ID)

    loads = [pltpu.make_async_copy(hbm[i], held[i], load_sem.at[i]) for i in range(13)]
    for i in (4, 1, 7, 3, 0, 8, 2, 5, 9, 10, 11, 12, 6):
        loads[i].start()

    loads[4].wait()
    lists[...] = jnp.zeros_like(lists)
    lists[0:1, 0:rim] = send_ref[0:1, :].astype(F32)
    lists[0:1, rim : 2 * rim] = send_ref[1:2, :].astype(F32)
    columns[...] = lists[...].T
    loads[1].wait()
    loads[7].wait()
    known[0:owned, :] = (0.5 * dot(mesh_ref[...], w_src_ref[...])).astype(BF)

    def select(side):
        rows = pl.ds(pl.multiple_of(side * rim, rim), rim)
        hot = one_hot_columns(columns[rows, 0:1].astype(jnp.int32), owned)
        return dot(hot, known[0:owned, :]).astype(BF)

    to_near = remote(
        out_halo.at[0], known.at[pl.ds(owned, rim)], halo_send.at[0], halo_recv.at[0], band=near_band
    )
    to_far = remote(out_halo.at[1], away.at[pl.ds(0, rim)], halo_send.at[1], halo_recv.at[1], band=far_band)
    out_halo[1] = select(far)
    pl.semaphore_wait(
        barrier, n_member - 1 + jnp.where(has_below, 1, 0) + jnp.where(has_above, 1, 0)
    )

    @pl.when(has_far)
    def _():
        to_far.start()

    out_halo[0] = select(near)
    to_near.start()

    @pl.when(jnp.logical_not(has_far))
    def _():
        away[0:rim, :] = jnp.zeros((rim, channels), BF)
        back[rim : 2 * rim, :] = jnp.zeros((rim, channels), BF)

    for i in (3, 2, 5, 9, 12, 6, 11):
        loads[i].wait()
    names = near_ref[...]
    in_near = (names >= owned + near * rim) & (names < owned + (near + 1) * rim)
    known_names = jnp.where(in_near, names - near * rim, jnp.where(names < owned, names, -1))
    wide[...] = jnp.zeros_like(wide)
    wide[0:fields, :] = target_ref[...]
    wide[COL_KNOWN : COL_KNOWN + edges, :] = known_names.astype(F32)
    wide[COL_FAR : COL_FAR + edges, :] = (names - owned - far * rim).astype(F32)
    for feature in range(features):
        wide[COL_EDGE + feature * edges : COL_EDGE + (feature + 1) * edges, :] = edge_ref[feature].astype(F32)
    table[...] = wide[...].T
    w_out[...] = jnp.zeros_like(w_out)
    w_out[0:fields, :] = w_out_ref[...]
    weights[...] = jnp.zeros_like(weights)
    weights[0:1, 0:fields] = weight_ref[...]
    away[rim:, :] = jnp.zeros((LANES, channels), BF)
    for feature in range(features):
        half = (0.5 * w_edge_ref[feature : feature + 1, :].astype(F32)).astype(BF)
        for edge in range(edges):
            row = rim + COL_EDGE + feature * edges + edge
            away[row : row + 1, :] = half
    loads[0].wait()
    loads[8].wait()
    zhat[...] = 0.5 * dot(grid_ref[...], w_dst_ref[...])
    to_near.wait_recv()

    def gather_known(part):
        rows = pl.ds(firsts[part], sizes[part])
        hot = jnp.concatenate(
            [
                one_hot_columns(
                    table[rows, COL_KNOWN + edge : COL_KNOWN + edge + 1].astype(jnp.int32), owned + rim
                )
                for edge in range(edges)
            ],
            axis=0,
        )
        found = dot(hot, known[...])
        dst = zhat[rows, :]
        for edge in range(edges):
            base[edge, rows, :] = found[edge * sizes[part] : (edge + 1) * sizes[part], :] + dst

    gather_known(0)
    gather_known(1)
    loads[10].wait()

    @pl.when(has_far)
    def _():
        to_far.wait_recv()

    gain = gain_ref[...]
    reads = (read_even, read_odd)

    def read(part):
        rows = pl.ds(firsts[part], sizes[part])
        lane = lax.broadcasted_iota(jnp.int32, (sizes[part], LANES), 1)
        values = table[rows, :]
        hots = []
        for edge in range(edges):
            column = table[rows, COL_FAR + edge : COL_FAR + edge + 1].astype(jnp.int32)
            chosen = (lane >= COL_EDGE) & (lane < COL_FAR) & (lax.rem(lane, edges) == edge)
            hots.append(
                jnp.concatenate(
                    [
                        one_hot_columns(column, rim),
                        jnp.where(chosen, values, 0.0).astype(BF),
                    ],
                    axis=1,
                )
            )
        reads[part % 2][0 : edges * sizes[part], :] = dot(jnp.concatenate(hots, axis=0), away[...])

    def forward(part):
        rows = pl.ds(firsts[part], sizes[part])
        total = None
        derivs = None
        for edge in range(edges):
            half = reads[part % 2][edge * sizes[part] : (edge + 1) * sizes[part], :] + base[edge, rows, :]
            rise = jnp.tanh(half) + 1.0
            act = half * rise
            twice = rise + act * (2.0 - rise)
            deriv[edge, rows, :] = twice.astype(BF)
            total = act if total is None else total + act
            derivs = twice if derivs is None else derivs + twice
        deriv_sum[rows, :] = derivs
        z = grid_ref[rows, :].astype(F32) + dot(total.astype(BF), w_msg_ref[...])
        centre = z - jnp.mean(z, axis=1, keepdims=True)
        scale = lax.rsqrt(jnp.mean(centre * centre, axis=1, keepdims=True) + LN_EPS)
        hat = centre * scale
        zhat[rows, :] = hat
        rstd[rows, :] = jnp.broadcast_to(scale, (sizes[part], LANES))
        pred[rows, :] = dot_t((hat * gain).astype(BF), w_out[...]).astype(BF)

    def pred_copy(part, other):
        return remote(
            pred.at[pl.ds(firsts[part] + other * shares[part], shares[part])],
            peers.at[me, pl.ds(owns[part], shares[part])],
            pred_send,
            pred_recv.at[part],
            member=other,
        )

    def grad_copy(part, other):
        return remote(
            d_peers.at[other, pl.ds(owns[part], shares[part])],
            d_pred.at[pl.ds(firsts[part] + me * shares[part], shares[part])],
            d_send,
            d_recv.at[part],
            member=other,
        )

    def all_of(count, send_sem, recv_sem):
        size = pl.ds(0, count)
        return remote(pred.at[size], d_pred.at[size], send_sem, recv_sem, member=lax.rem(me + 1, n_member))

    def send_pred(part):
        for other in others():
            pred_copy(part, other).start()
        mine = pl.ds(pl.multiple_of(firsts[part] + me * shares[part], 16), shares[part])
        peers[me, pl.ds(owns[part], shares[part]), :] = pred[mine, :]

    def compare(part):
        all_of((n_member - 1) * shares[part], pred_send, pred_recv.at[part]).wait_recv()
        share = shares[part]
        rows = pl.ds(owns[part], share)
        mine = pl.ds(pl.multiple_of(firsts[part] + me * share, 16), share)
        goal = table[mine, :]
        lane = lax.broadcasted_iota(jnp.int32, (share, LANES), 1)
        goal = jnp.where(lane < fields, goal, 0.0)
        values = [peers[member, rows, :].astype(F32) for member in range(n_member)]
        spread = [jnp.zeros((share, LANES), F32) for _ in range(n_member)]
        for left in range(n_member):
            for right in range(left + 1, n_member):
                step = slope(values[left] - values[right])
                spread[left] = spread[left] + step
                spread[right] = spread[right] - step
        for member in range(n_member):
            grad = weights[...] * (slope(values[member] - goal) - coeff * spread[member])
            d_peers[member, rows, :] = grad.astype(BF)
        for other in others():
            grad_copy(part, other).start()
        d_pred[mine, :] = d_peers[me, rows, :]

    def backward(part):
        all_of((n_member - 1) * shares[part], d_send, d_recv.at[part]).wait_recv()
        rows = pl.ds(firsts[part], sizes[part])
        hat = zhat[rows, :]
        scale = rstd[rows, 0:1]
        scaled = dot(d_pred[rows, :], w_out[...]) * gain
        d_z = scale * (
            scaled
            - jnp.mean(scaled, axis=1, keepdims=True)
            - hat * jnp.mean(scaled * hat, axis=1, keepdims=True)
        )
        zhat[rows, :] = d_z
        d_act = 0.5 * dot_t(d_z.astype(BF), w_msg_ref[...])
        d_sum[rows, :] = (d_act * deriv_sum[rows, :]).astype(BF)
        d_act = d_act.astype(BF)
        for edge in range(edges):
            deriv[edge, rows, :] = d_act * deriv[edge, rows, :]

    def scatter(first_part, last_part, first, height):
        rows = pl.ds(firsts[first_part], firsts[last_part] + sizes[last_part] - firsts[first_part])
        names = jnp.concatenate([near_ref[edge : edge + 1, rows] for edge in range(edges)], axis=1)
        grads = jnp.concatenate([deriv[edge, rows, :] for edge in range(edges)], axis=0)
        return dot(one_hot_rows(names, height, first), grads)

    def scatter_far(part):
        return scatter(part, part, owned + far * rim, rim)

    read(0)
    forward(0)
    send_pred(0)
    read(1)
    forward(1)
    send_pred(1)
    compare(0)
    gather_known(2)
    read(2)
    forward(2)
    send_pred(2)
    compare(1)
    backward(0)
    rims[...] = scatter_far(0)
    slots[...] = scatter(0, 0, 0, owned)
    compare(2)
    backward(1)
    rims[...] += scatter_far(1)
    slots[...] += scatter(1, 1, 0, owned)
    backward(2)
    d_halo[1] = (rims[...] + scatter_far(2)).astype(BF)

    back_near = remote(
        d_halo.at[0], back.at[pl.ds(0, rim)], back_send.at[0], back_recv.at[0], band=near_band
    )
    back_far = remote(
        d_halo.at[1], back.at[pl.ds(rim, rim)], back_send.at[1], back_recv.at[1], band=far_band
    )

    @pl.when(has_far)
    def _():
        back_far.start()

    d_halo[0] = scatter(0, 2, owned + near * rim, rim).astype(BF)
    back_near.start()
    d_grid[...] = (zhat[...] + dot_t(d_sum[...], w_dst_ref[...])).astype(BF)
    slots[...] += scatter(2, 2, 0, owned)

    def returned(side, place):
        return dot(
            one_hot_rows(send_ref[pl.ds(side, 1), :], owned, 0), back[place * rim : (place + 1) * rim, :]
        )

    back_near.wait_recv()
    slots[...] += returned(near, 0)

    @pl.when(has_far)
    def _():
        back_far.wait_recv()

    sums[...] = (slots[...] + returned(far, 1)).astype(BF)

    to_near.wait_send()
    back_near.wait_send()

    @pl.when(has_far)
    def _():
        to_far.wait_send()
        back_far.wait_send()

    all_of((n_member - 1) * sum(shares), pred_send, pred_recv.at[0]).wait_send()
    all_of((n_member - 1) * sum(shares), d_send, d_recv.at[0]).wait_send()


def finish(d_grid, sums, w_src, grid_out, mesh_out, rows_out, store_sem):
    through = pltpu.make_async_copy(d_grid, grid_out, store_sem.at[0])
    through.start()
    height = sums.shape[0] // 2
    stores = []
    for part in range(2):
        rows = pl.ds(part * height, height)
        rows_out[rows, :] = dot_t(sums[rows, :], w_src[...]).astype(BF)
        stores.append(
            pltpu.make_async_copy(rows_out.at[rows], mesh_out.at[rows], store_sem.at[part + 1])
        )
        stores[-1].start()
    through.wait()
    for store in stores:
        store.wait()


def per_device(
    n_band,
    n_member,
    grid_latent,
    mesh_latent,
    edge_attr,
    neighbours,
    send_rows,
    target,
    field_weight,
    w_src,
    w_dst,
    w_edge,
    w_msg,
    ln_gain,
    w_out,
):
    grid_rows = grid_latent[0]
    mesh_rows = mesh_latent[0]
    points, channels = grid_rows.shape
    owned = mesh_rows.shape[0]
    edges = neighbours.shape[1]
    rim = send_rows.shape[1]
    fields = target.shape[0]
    share = points // n_member
    largest = max(PARTS) * UNIT
    operands = (
        grid_rows,
        mesh_rows,
        edge_attr,
        neighbours.T,
        send_rows,
        target,
        field_weight.reshape(1, fields),
        w_src,
        w_dst,
        w_edge,
        w_msg,
        ln_gain.reshape(1, channels),
        w_out.T,
    )
    anywhere = pl.BlockSpec(memory_space=pl.ANY)
    vmem = pl.BlockSpec(memory_space=pltpu.VMEM)
    dma = pltpu.SemaphoreType.DMA
    latents = pltpu.VMEM((points, channels), BF)
    wide_latents = pltpu.VMEM((points, channels), F32)
    d_grid, sums = pl.pallas_call(
        functools.partial(kernel, n_band, n_member),
        out_shape=(pltpu.VMEM((points, channels), BF), pltpu.VMEM((owned, channels), BF)),
        in_specs=[anywhere] * len(operands),
        out_specs=(vmem, vmem),
        scratch_shapes=[pltpu.VMEM(operand.shape, operand.dtype) for operand in operands]
        + [
            pltpu.VMEM((8, 2 * rim), F32),
            pltpu.VMEM((LANES, points), F32),
            pltpu.VMEM((points, LANES), F32),
            pltpu.VMEM((LANES, channels), BF),
            pltpu.VMEM((1, LANES), F32),
            pltpu.VMEM((2 * rim, 8), F32),
            pltpu.VMEM((owned + rim, channels), BF),
            pltpu.VMEM((2, rim, channels), BF),
            pltpu.VMEM((rim + LANES, channels), BF),
            pltpu.VMEM((edges, points, channels), F32),
            pltpu.VMEM((edges * largest, channels), F32),
            pltpu.VMEM((edges * largest, channels), F32),
            pltpu.VMEM((edges, points, channels), BF),
            wide_latents,
            wide_latents,
            pltpu.VMEM((points, LANES), F32),
            pltpu.VMEM((points, LANES), BF),
            pltpu.VMEM((n_member, share, LANES), BF),
            pltpu.VMEM((n_member, share, LANES), BF),
            pltpu.VMEM((points, LANES), BF),
            latents,
            wide_latents,
            pltpu.VMEM((rim, channels), F32),
            pltpu.VMEM((2, rim, channels), BF),
            pltpu.VMEM((2 * rim, channels), BF),
            dma((len(operands),)),
            dma((2,)),
            dma((2,)),
            dma,
            dma((len(PARTS),)),
            dma,
            dma((len(PARTS),)),
            dma((2,)),
            dma((2,)),
        ],
        compiler_params=pltpu.CompilerParams(
            collective_id=0, has_side_effects=True, vmem_limit_bytes=52 * 2**20
        ),
    )(*operands)
    d_grid, d_mesh = pl.pallas_call(
        finish,
        out_shape=(
            jax.ShapeDtypeStruct((points, channels), BF),
            jax.ShapeDtypeStruct((owned, channels), BF),
        ),
        in_specs=[vmem] * 3,
        out_specs=(anywhere, anywhere),
        scratch_shapes=[latents, dma((3,))],
        compiler_params=pltpu.CompilerParams(vmem_limit_bytes=16 * 2**20),
    )(d_grid, sums, w_src)
    return d_grid[None], d_mesh[None]


def solution(mesh):
    placed = (
        P("member", "band", None),
        P("member", "band", None),
        P(None, None, "band"),
        P("band", None),
        P("band", None),
        P(None, "band"),
        P(),
        P(),
        P(),
        P(),
        P(),
        P(),
        P(),
    )
    return jax.shard_map(
        functools.partial(per_device, mesh.shape["band"], mesh.shape["member"]),
        mesh=mesh,
        in_specs=placed,
        out_specs=(P("member", "band", None), P("member", "band", None)),
        check_vma=False,
    )
```

```python
import functools

import jax
import jax.numpy as jnp
from jax import lax
from jax.experimental import pallas as pl
from jax.experimental.pallas import tpu as pltpu
from jax.sharding import PartitionSpec as P

DELTA_SQ = 0.0625
ALPHA = 0.95
LN_EPS = 1e-05

BF = jnp.bfloat16
F32 = jnp.float32
LANES = 128
PARTS = (3, 3, 2)
UNIT = 128
MESH_ID = pl.DeviceIdType.MESH

COL_KNOWN = 100
COL_EDGE = 104
COL_FAR = 120


def dot(left, right):
    return jnp.dot(left, right, preferred_element_type=F32)


def dot_t(left, right):
    return lax.dot_general(left, right, (((1,), (1,)), ((), ())), preferred_element_type=F32)


def slope(diff):
    return diff * lax.rsqrt(diff * diff + DELTA_SQ)


def one_hot_columns(column, width):
    rows = column.shape[0]
    return jnp.where(lax.broadcasted_iota(jnp.int32, (rows, width), 1) == column, 1.0, 0.0).astype(BF)


def one_hot_rows(row, height, first):
    width = row.shape[1]
    return jnp.where(
        lax.broadcasted_iota(jnp.int32, (height, width), 0) + first == row, 1.0, 0.0
    ).astype(BF)


def remote(src, dst, send_sem, recv_sem, **where):
    return pltpu.make_async_remote_copy(
        src_ref=src, dst_ref=dst, send_sem=send_sem, recv_sem=recv_sem, device_id=where, device_id_type=MESH_ID
    )


def kernel(n_band, n_member, *refs):
    hbm, (d_grid, sums), refs = refs[:13], refs[13:15], refs[15:]
    held, refs = refs[:13], refs[13:]
    (
        grid_ref,
        mesh_ref,
        edge_ref,
        near_ref,
        send_ref,
        target_ref,
        weight_ref,
        w_src_ref,
        w_dst_ref,
        w_edge_ref,
        w_msg_ref,
        gain_ref,
        w_out_ref,
    ) = held
    (
        lists,
        wide,
        table,
        w_out,
        weights,
        columns,
        known,
        out_halo,
        away,
        base,
        read_even,
        read_odd,
        deriv,
        deriv_sum,
        zhat,
        rstd,
        pred,
        peers,
        d_peers,
        d_pred,
        d_sum,
        slots,
        rims,
        d_halo,
        back,
        load_sem,
        halo_send,
        halo_recv,
        pred_send,
        pred_recv,
        d_send,
        d_recv,
        back_send,
        back_recv,
    ) = refs
    points, channels = grid_ref.shape
    owned = mesh_ref.shape[0]
    features = edge_ref.shape[0]
    edges = near_ref.shape[0]
    rim = send_ref.shape[1]
    fields = target_ref.shape[0]
    firsts = [sum(PARTS[:part]) * UNIT for part in range(len(PARTS))]
    sizes = [part * UNIT for part in PARTS]
    shares = [size // n_member for size in sizes]
    owns = [first // n_member for first in firsts]
    band = lax.axis_index("band")
    me = lax.axis_index("member")
    has_below = band > 0
    has_above = band < n_band - 1
    far = lax.rem(band, 2)
    near = 1 - far
    has_far = ((far == 0) & has_below) | ((far == 1) & has_above)
    near_band = band + 2 * near - 1
    far_band = jnp.clip(band + 2 * far - 1, 0, n_band - 1)
    coeff = ALPHA / (n_member - 1) + (1.0 - ALPHA) / n_member

    def others():
        ring = n_member // 2
        along, row = lax.rem(me, ring), me // ring
        hops = sorted(
            ((dy, dx) for dy in range(2) for dx in range(ring) if dy + dx > 0),
            key=lambda hop: -(hop[0] + min(hop[1], ring - hop[1])),
        )
        return [lax.rem(row + dy, 2) * ring + lax.rem(along + dx, ring) for dy, dx in hops]

    barrier = pltpu.get_barrier_semaphore()

    @pl.when(has_below)
    def _():
        pl.semaphore_signal(barrier, inc=1, device_id={"band": band - 1}, device_id_type=MESH_ID)

    @pl.when(has_above)
    def _():
        pl.semaphore_signal(barrier, inc=1, device_id={"band": band + 1}, device_id_type=MESH_ID)

    for other in others():
        pl.semaphore_signal(barrier, inc=1, device_id={"member": other}, device_id_type=MESH_ID)

    loads = [pltpu.make_async_copy(hbm[i], held[i], load_sem.at[i]) for i in range(13)]
    for i in (4, 7, 1):
        loads[i].start()

    loads[4].wait()
    lists[...] = jnp.zeros_like(lists)
    lists[0:1, 0:rim] = send_ref[0:1, :].astype(F32)
    lists[0:1, rim : 2 * rim] = send_ref[1:2, :].astype(F32)
    columns[...] = lists[...].T
    loads[7].wait()
    loads[1].wait()
    for i in (3, 2, 5, 9, 12, 6, 11, 0, 8, 10):
        loads[i].start()
    known[0:owned, :] = (0.5 * dot(mesh_ref[...], w_src_ref[...])).astype(BF)

    halves = (pl.ds(0, rim // 2), pl.ds(rim // 2, rim // 2))

    def select(side, first, count):
        rows = pl.ds(pl.multiple_of(side * rim + first, count), count)
        hot = one_hot_columns(columns[rows, 0:1].astype(jnp.int32), owned)
        return dot(hot, known[0:owned, :]).astype(BF)

    to_near = remote(
        out_halo.at[0], known.at[pl.ds(owned, rim)], halo_send.at[0], halo_recv.at[0], band=near_band
    )
    to_far = [
        remote(
            out_halo.at[1, rows], away.at[rows], halo_send.at[1 + i], halo_recv.at[1 + i], band=far_band
        )
        for i, rows in enumerate(halves)
    ]
    out_halo[1, halves[0], :] = select(far, 0, rim // 2)
    pl.semaphore_wait(
        barrier, n_member - 1 + jnp.where(has_below, 1, 0) + jnp.where(has_above, 1, 0)
    )

    @pl.when(has_far)
    def _():
        to_far[0].start()

    out_halo[1, halves[1], :] = select(far, rim // 2, rim // 2)

    @pl.when(has_far)
    def _():
        to_far[1].start()

    out_halo[0] = select(near, 0, rim)
    to_near.start()

    @pl.when(jnp.logical_not(has_far))
    def _():
        away[0:rim, :] = jnp.zeros((rim, channels), BF)
        back[rim : 2 * rim, :] = jnp.zeros((rim, channels), BF)

    for i in (3, 2, 5, 9, 12, 6, 11):
        loads[i].wait()
    names = near_ref[...]
    in_near = (names >= owned + near * rim) & (names < owned + (near + 1) * rim)
    known_names = jnp.where(in_near, names - near * rim, jnp.where(names < owned, names, -1))
    wide[...] = jnp.zeros_like(wide)
    wide[0:fields, :] = target_ref[...]
    wide[COL_KNOWN : COL_KNOWN + edges, :] = known_names.astype(F32)
    wide[COL_FAR : COL_FAR + edges, :] = (names - owned - far * rim).astype(F32)
    for feature in range(features):
        wide[COL_EDGE + feature * edges : COL_EDGE + (feature + 1) * edges, :] = edge_ref[feature].astype(F32)
    table[...] = wide[...].T
    w_out[...] = jnp.zeros_like(w_out)
    w_out[0:fields, :] = w_out_ref[...]
    weights[...] = jnp.zeros_like(weights)
    weights[0:1, 0:fields] = weight_ref[...]
    known[owned + rim :, :] = jnp.zeros((LANES, channels), BF)
    for feature in range(features):
        half = (0.5 * w_edge_ref[feature : feature + 1, :].astype(F32)).astype(BF)
        for edge in range(edges):
            row = owned + rim + COL_EDGE + feature * edges + edge
            known[row : row + 1, :] = half
    loads[0].wait()
    loads[8].wait()
    zhat[...] = 0.5 * dot(grid_ref[...], w_dst_ref[...])
    to_near.wait_recv()

    def gather_known(part):
        rows = pl.ds(firsts[part], sizes[part])
        lane = lax.broadcasted_iota(jnp.int32, (sizes[part], LANES), 1)
        values = table[rows, :]
        hots = []
        for edge in range(edges):
            column = table[rows, COL_KNOWN + edge : COL_KNOWN + edge + 1].astype(jnp.int32)
            chosen = (lane >= COL_EDGE) & (lane < COL_FAR) & (lax.rem(lane, edges) == edge)
            hots.append(
                jnp.concatenate(
                    [
                        one_hot_columns(column, owned + rim),
                        jnp.where(chosen, values, 0.0).astype(BF),
                    ],
                    axis=1,
                )
            )
        found = dot(jnp.concatenate(hots, axis=0), known[...])
        dst = zhat[rows, :]
        for edge in range(edges):
            base[edge, rows, :] = found[edge * sizes[part] : (edge + 1) * sizes[part], :] + dst

    gather_known(0)
    gather_known(1)
    gather_known(2)
    loads[10].wait()

    @pl.when(has_far)
    def _():
        to_far[0].wait_recv()
        to_far[1].wait_recv()

    gain = gain_ref[...]
    reads = (read_even, read_odd)

    def read(part):
        rows = pl.ds(firsts[part], sizes[part])
        hots = [
            one_hot_columns(table[rows, COL_FAR + edge : COL_FAR + edge + 1].astype(jnp.int32), rim)
            for edge in range(edges)
        ]
        found = dot(jnp.concatenate(hots, axis=0), away[...])
        reads[part % 2][0 : edges * sizes[part], :] = found

    def forward(part):
        rows = pl.ds(firsts[part], sizes[part])
        total = None
        for edge in range(edges):
            half = reads[part % 2][edge * sizes[part] : (edge + 1) * sizes[part], :] + base[edge, rows, :]
            base[edge, rows, :] = half
            act = half * (jnp.tanh(half) + 1.0)
            total = act if total is None else total + act
        z = grid_ref[rows, :].astype(F32) + dot(total.astype(BF), w_msg_ref[...])
        centre = z - jnp.mean(z, axis=1, keepdims=True)
        scale = lax.rsqrt(jnp.mean(centre * centre, axis=1, keepdims=True) + LN_EPS)
        hat = centre * scale
        zhat[rows, :] = hat
        rstd[rows, :] = jnp.broadcast_to(scale, (sizes[part], LANES))
        pred[rows, :] = dot_t((hat * gain).astype(BF), w_out[...]).astype(BF)

    def derive(part):
        rows = pl.ds(firsts[part], sizes[part])
        total = None
        for edge in range(edges):
            half = base[edge, rows, :]
            rise = jnp.tanh(half) + 1.0
            twice = rise + half * rise * (2.0 - rise)
            deriv[edge, rows, :] = twice.astype(BF)
            total = twice if total is None else total + twice
        deriv_sum[rows, :] = total

    def pred_copy(part, other):
        return remote(
            pred.at[pl.ds(firsts[part] + other * shares[part], shares[part])],
            peers.at[me, pl.ds(owns[part], shares[part])],
            pred_send,
            pred_recv.at[part],
            member=other,
        )

    def grad_copy(part, other):
        return remote(
            d_peers.at[other, pl.ds(owns[part], shares[part])],
            d_pred.at[pl.ds(firsts[part] + me * shares[part], shares[part])],
            d_send,
            d_recv.at[part],
            member=other,
        )

    def all_of(count, send_sem, recv_sem):
        size = pl.ds(0, count)
        return remote(pred.at[size], d_pred.at[size], send_sem, recv_sem, member=lax.rem(me + 1, n_member))

    def send_pred(part):
        for other in others():
            pred_copy(part, other).start()
        mine = pl.ds(pl.multiple_of(firsts[part] + me * shares[part], 16), shares[part])
        peers[me, pl.ds(owns[part], shares[part]), :] = pred[mine, :]

    def compare(part):
        all_of((n_member - 1) * shares[part], pred_send, pred_recv.at[part]).wait_recv()
        share = shares[part]
        rows = pl.ds(owns[part], share)
        mine = pl.ds(pl.multiple_of(firsts[part] + me * share, 16), share)
        goal = table[mine, :]
        lane = lax.broadcasted_iota(jnp.int32, (share, LANES), 1)
        goal = jnp.where(lane < fields, goal, 0.0)
        values = [peers[member, rows, :].astype(F32) for member in range(n_member)]
        spread = [jnp.zeros((share, LANES), F32) for _ in range(n_member)]
        for left in range(n_member):
            for right in range(left + 1, n_member):
                step = slope(values[left] - values[right])
                spread[left] = spread[left] + step
                spread[right] = spread[right] - step
        for member in range(n_member):
            grad = weights[...] * (slope(values[member] - goal) - coeff * spread[member])
            d_peers[member, rows, :] = grad.astype(BF)
        for other in others():
            grad_copy(part, other).start()
        d_pred[mine, :] = d_peers[me, rows, :]

    def backward(part):
        all_of((n_member - 1) * shares[part], d_send, d_recv.at[part]).wait_recv()
        rows = pl.ds(firsts[part], sizes[part])
        hat = zhat[rows, :]
        scale = rstd[rows, 0:1]
        scaled = dot(d_pred[rows, :], w_out[...]) * gain
        d_z = scale * (
            scaled
            - jnp.mean(scaled, axis=1, keepdims=True)
            - hat * jnp.mean(scaled * hat, axis=1, keepdims=True)
        )
        zhat[rows, :] = d_z
        d_act = 0.5 * dot_t(d_z.astype(BF), w_msg_ref[...])
        d_sum[rows, :] = (d_act * deriv_sum[rows, :]).astype(BF)
        d_act = d_act.astype(BF)
        for edge in range(edges):
            deriv[edge, rows, :] = d_act * deriv[edge, rows, :]

    def scatter(first_part, last_part, first, height):
        rows = pl.ds(firsts[first_part], firsts[last_part] + sizes[last_part] - firsts[first_part])
        names = jnp.concatenate([near_ref[edge : edge + 1, rows] for edge in range(edges)], axis=1)
        grads = jnp.concatenate([deriv[edge, rows, :] for edge in range(edges)], axis=0)
        return dot(one_hot_rows(names, height, first), grads)

    def scatter_far(part, first, count):
        return scatter(part, part, owned + far * rim + first, count)

    read(0)
    forward(0)
    send_pred(0)
    read(1)
    forward(1)
    send_pred(1)
    read(2)
    forward(2)
    send_pred(2)
    compare(0)
    derive(0)
    compare(1)
    derive(1)
    derive(2)
    compare(2)
    backward(0)
    rims[...] = scatter_far(0, 0, rim)
    backward(1)
    rims[...] += scatter_far(1, 0, rim)
    backward(2)
    back_near = remote(
        d_halo.at[0], back.at[pl.ds(0, rim)], back_send.at[0], back_recv.at[0], band=near_band
    )
    back_far = [
        remote(
            d_halo.at[1, rows],
            back.at[pl.ds(rim + i * (rim // 2), rim // 2)],
            back_send.at[1 + i],
            back_recv.at[1 + i],
            band=far_band,
        )
        for i, rows in enumerate(halves)
    ]
    d_halo[1, halves[0], :] = (rims[halves[0], :] + scatter_far(2, 0, rim // 2)).astype(BF)

    @pl.when(has_far)
    def _():
        back_far[0].start()

    d_halo[1, halves[1], :] = (rims[halves[1], :] + scatter_far(2, rim // 2, rim // 2)).astype(BF)

    @pl.when(has_far)
    def _():
        back_far[1].start()

    d_halo[0] = scatter(0, 2, owned + near * rim, rim).astype(BF)
    back_near.start()
    d_grid[...] = (zhat[...] + dot_t(d_sum[...], w_dst_ref[...])).astype(BF)
    slots[...] = scatter(0, 2, 0, owned)

    def returned(side, first, place, count):
        names = send_ref[pl.ds(side, 1), pl.ds(first, count)]
        return dot(one_hot_rows(names, owned, 0), back[pl.ds(place, count), :])

    back_near.wait_recv()
    slots[...] += returned(near, 0, 0, rim)

    @pl.when(has_far)
    def _():
        back_far[0].wait_recv()

    slots[...] += returned(far, 0, rim, rim // 2)

    @pl.when(has_far)
    def _():
        back_far[1].wait_recv()

    sums[...] = (slots[...] + returned(far, rim // 2, rim + rim // 2, rim // 2)).astype(BF)

    to_near.wait_send()
    back_near.wait_send()

    @pl.when(has_far)
    def _():
        for copy in to_far + back_far:
            copy.wait_send()

    all_of((n_member - 1) * sum(shares), pred_send, pred_recv.at[0]).wait_send()
    all_of((n_member - 1) * sum(shares), d_send, d_recv.at[0]).wait_send()


def finish(d_grid, sums, w_src, grid_out, mesh_out, rows_out, store_sem):
    through = pltpu.make_async_copy(d_grid, grid_out, store_sem.at[0])
    through.start()
    height = sums.shape[0] // 2
    stores = []
    for part in range(2):
        rows = pl.ds(part * height, height)
        rows_out[rows, :] = dot_t(sums[rows, :], w_src[...]).astype(BF)
        stores.append(
            pltpu.make_async_copy(rows_out.at[rows], mesh_out.at[rows], store_sem.at[part + 1])
        )
        stores[-1].start()
    through.wait()
    for store in stores:
        store.wait()


def per_device(
    n_band,
    n_member,
    grid_latent,
    mesh_latent,
    edge_attr,
    neighbours,
    send_rows,
    target,
    field_weight,
    w_src,
    w_dst,
    w_edge,
    w_msg,
    ln_gain,
    w_out,
):
    grid_rows = grid_latent[0]
    mesh_rows = mesh_latent[0]
    points, channels = grid_rows.shape
    owned = mesh_rows.shape[0]
    edges = neighbours.shape[1]
    rim = send_rows.shape[1]
    fields = target.shape[0]
    share = points // n_member
    largest = max(PARTS) * UNIT
    operands = (
        grid_rows,
        mesh_rows,
        edge_attr,
        neighbours.T,
        send_rows,
        target,
        field_weight.reshape(1, fields),
        w_src,
        w_dst,
        w_edge,
        w_msg,
        ln_gain.reshape(1, channels),
        w_out.T,
    )
    anywhere = pl.BlockSpec(memory_space=pl.ANY)
    vmem = pl.BlockSpec(memory_space=pltpu.VMEM)
    dma = pltpu.SemaphoreType.DMA
    latents = pltpu.VMEM((points, channels), BF)
    wide_latents = pltpu.VMEM((points, channels), F32)
    d_grid, sums = pl.pallas_call(
        functools.partial(kernel, n_band, n_member),
        out_shape=(pltpu.VMEM((points, channels), BF), pltpu.VMEM((owned, channels), BF)),
        in_specs=[anywhere] * len(operands),
        out_specs=(vmem, vmem),
        scratch_shapes=[pltpu.VMEM(operand.shape, operand.dtype) for operand in operands]
        + [
            pltpu.VMEM((8, 2 * rim), F32),
            pltpu.VMEM((LANES, points), F32),
            pltpu.VMEM((points, LANES), F32),
            pltpu.VMEM((LANES, channels), BF),
            pltpu.VMEM((1, LANES), F32),
            pltpu.VMEM((2 * rim, 8), F32),
            pltpu.VMEM((owned + rim + LANES, channels), BF),
            pltpu.VMEM((2, rim, channels), BF),
            pltpu.VMEM((rim, channels), BF),
            pltpu.VMEM((edges, points, channels), F32),
            pltpu.VMEM((edges * largest, channels), F32),
            pltpu.VMEM((edges * largest, channels), F32),
            pltpu.VMEM((edges, points, channels), BF),
            wide_latents,
            wide_latents,
            pltpu.VMEM((points, LANES), F32),
            pltpu.VMEM((points, LANES), BF),
            pltpu.VMEM((n_member, share, LANES), BF),
            pltpu.VMEM((n_member, share, LANES), BF),
            pltpu.VMEM((points, LANES), BF),
            latents,
            wide_latents,
            pltpu.VMEM((rim, channels), F32),
            pltpu.VMEM((2, rim, channels), BF),
            pltpu.VMEM((2 * rim, channels), BF),
            dma((len(operands),)),
            dma((3,)),
            dma((3,)),
            dma,
            dma((len(PARTS),)),
            dma,
            dma((len(PARTS),)),
            dma((3,)),
            dma((3,)),
        ],
        compiler_params=pltpu.CompilerParams(
            collective_id=0, has_side_effects=True, vmem_limit_bytes=52 * 2**20
        ),
    )(*operands)
    d_grid, d_mesh = pl.pallas_call(
        finish,
        out_shape=(
            jax.ShapeDtypeStruct((points, channels), BF),
            jax.ShapeDtypeStruct((owned, channels), BF),
        ),
        in_specs=[vmem] * 3,
        out_specs=(anywhere, anywhere),
        scratch_shapes=[latents, dma((3,))],
        compiler_params=pltpu.CompilerParams(vmem_limit_bytes=16 * 2**20),
    )(d_grid, sums, w_src)
    return d_grid[None], d_mesh[None]


def solution(mesh):
    placed = (
        P("member", "band", None),
        P("member", "band", None),
        P(None, None, "band"),
        P("band", None),
        P("band", None),
        P(None, "band"),
        P(),
        P(),
        P(),
        P(),
        P(),
        P(),
        P(),
    )
    return jax.shard_map(
        functools.partial(per_device, mesh.shape["band"], mesh.shape["member"]),
        mesh=mesh,
        in_specs=placed,
        out_specs=(P("member", "band", None), P("member", "band", None)),
        check_vma=False,
    )
```

```python
import functools

import jax
import jax.numpy as jnp
from jax import lax
from jax.experimental import pallas as pl
from jax.experimental.pallas import tpu as pltpu
from jax.sharding import PartitionSpec as P

DELTA_SQ = 0.0625
ALPHA = 0.95
LN_EPS = 1e-05

BF = jnp.bfloat16
F32 = jnp.float32
LANES = 128
PARTS = (3, 3, 2)
UNIT = 128
MESH_ID = pl.DeviceIdType.MESH

COL_KNOWN = 100
COL_EDGE = 104
COL_FAR = 120


def dot(left, right):
    return jnp.dot(left, right, preferred_element_type=F32)


def dot_t(left, right):
    return lax.dot_general(left, right, (((1,), (1,)), ((), ())), preferred_element_type=F32)


def slope(diff):
    return diff * lax.rsqrt(diff * diff + DELTA_SQ)


def one_hot_columns(column, width):
    rows = column.shape[0]
    return jnp.where(lax.broadcasted_iota(jnp.int32, (rows, width), 1) == column, 1.0, 0.0).astype(BF)


def one_hot_rows(row, height, first):
    width = row.shape[1]
    return jnp.where(
        lax.broadcasted_iota(jnp.int32, (height, width), 0) + first == row, 1.0, 0.0
    ).astype(BF)


def remote(src, dst, send_sem, recv_sem, **where):
    return pltpu.make_async_remote_copy(
        src_ref=src, dst_ref=dst, send_sem=send_sem, recv_sem=recv_sem, device_id=where, device_id_type=MESH_ID
    )


def kernel(n_band, n_member, *refs):
    hbm, (d_grid, sums), refs = refs[:13], refs[13:15], refs[15:]
    held, refs = refs[:13], refs[13:]
    (
        grid_ref,
        mesh_ref,
        edge_ref,
        near_ref,
        send_ref,
        target_ref,
        weight_ref,
        w_src_ref,
        w_dst_ref,
        w_edge_ref,
        w_msg_ref,
        gain_ref,
        w_out_ref,
    ) = held
    (
        lists,
        wide,
        table,
        w_out,
        weights,
        columns,
        known,
        out_halo,
        away,
        base,
        deriv,
        deriv_sum,
        zhat,
        rstd,
        pred,
        peers,
        d_peers,
        d_pred,
        d_sum,
        slots,
        rims,
        d_halo,
        back,
        load_sem,
        halo_send,
        halo_recv,
        pred_send,
        pred_recv,
        d_send,
        d_recv,
        back_send,
        back_recv,
    ) = refs
    points, channels = grid_ref.shape
    owned = mesh_ref.shape[0]
    features = edge_ref.shape[0]
    edges = near_ref.shape[0]
    rim = send_ref.shape[1]
    fields = target_ref.shape[0]
    firsts = [sum(PARTS[:part]) * UNIT for part in range(len(PARTS))]
    sizes = [part * UNIT for part in PARTS]
    shares = [size // n_member for size in sizes]
    owns = [first // n_member for first in firsts]
    band = lax.axis_index("band")
    me = lax.axis_index("member")
    has_below = band > 0
    has_above = band < n_band - 1
    far = lax.rem(band, 2)
    near = 1 - far
    has_far = ((far == 0) & has_below) | ((far == 1) & has_above)
    near_band = band + 2 * near - 1
    far_band = jnp.clip(band + 2 * far - 1, 0, n_band - 1)
    coeff = ALPHA / (n_member - 1) + (1.0 - ALPHA) / n_member

    def others():
        ring = n_member // 2
        along, row = lax.rem(me, ring), me // ring
        hops = sorted(
            ((dy, dx) for dy in range(2) for dx in range(ring) if dy + dx > 0),
            key=lambda hop: -(hop[0] + min(hop[1], ring - hop[1])),
        )
        return [lax.rem(row + dy, 2) * ring + lax.rem(along + dx, ring) for dy, dx in hops]

    barrier = pltpu.get_barrier_semaphore()

    @pl.when(has_below)
    def _():
        pl.semaphore_signal(barrier, inc=1, device_id={"band": band - 1}, device_id_type=MESH_ID)

    @pl.when(has_above)
    def _():
        pl.semaphore_signal(barrier, inc=1, device_id={"band": band + 1}, device_id_type=MESH_ID)

    for other in others():
        pl.semaphore_signal(barrier, inc=1, device_id={"member": other}, device_id_type=MESH_ID)

    loads = [pltpu.make_async_copy(hbm[i], held[i], load_sem.at[i]) for i in range(13)]
    for i in (4, 1, 7):
        loads[i].start()

    loads[4].wait()
    lists[...] = jnp.zeros_like(lists)
    lists[0:1, 0:rim] = send_ref[0:1, :].astype(F32)
    lists[0:1, rim : 2 * rim] = send_ref[1:2, :].astype(F32)
    columns[...] = lists[...].T
    halves = (pl.ds(0, rim // 2), pl.ds(rim // 2, rim // 2))

    def project(rows):
        return (0.5 * dot(rows, w_src_ref[...])).astype(BF)

    def select(source, side, first, count):
        rows = pl.ds(pl.multiple_of(side * rim + first, count), count)
        hot = one_hot_columns(columns[rows, 0:1].astype(jnp.int32), owned)
        return dot(hot, source[0:owned, :]).astype(BF)

    to_near = remote(
        out_halo.at[0], known.at[pl.ds(owned, rim)], halo_send.at[0], halo_recv.at[0], band=near_band
    )
    to_far = [
        remote(
            out_halo.at[1, rows], away.at[rows], halo_send.at[1 + i], halo_recv.at[1 + i], band=far_band
        )
        for i, rows in enumerate(halves)
    ]
    loads[1].wait()
    picked = select(mesh_ref, far, 0, rim // 2)
    loads[7].wait()
    for i in (3, 2, 5, 9, 12, 6, 11, 0, 8, 10):
        loads[i].start()
    out_halo[1, halves[0], :] = project(picked)
    pl.semaphore_wait(
        barrier, n_member - 1 + jnp.where(has_below, 1, 0) + jnp.where(has_above, 1, 0)
    )

    @pl.when(has_far)
    def _():
        to_far[0].start()

    out_halo[1, halves[1], :] = project(select(mesh_ref, far, rim // 2, rim // 2))

    @pl.when(has_far)
    def _():
        to_far[1].start()

    known[0:owned, :] = project(mesh_ref[...])
    out_halo[0] = select(known, near, 0, rim)
    to_near.start()

    @pl.when(jnp.logical_not(has_far))
    def _():
        away[0:rim, :] = jnp.zeros((rim, channels), BF)
        back[rim : 2 * rim, :] = jnp.zeros((rim, channels), BF)

    for i in (3, 2, 5, 9, 12, 6, 11):
        loads[i].wait()
    names = near_ref[...]
    in_near = (names >= owned + near * rim) & (names < owned + (near + 1) * rim)
    known_names = jnp.where(in_near, names - near * rim, jnp.where(names < owned, names, -1))
    wide[...] = jnp.zeros_like(wide)
    wide[0:fields, :] = target_ref[...]
    wide[COL_KNOWN : COL_KNOWN + edges, :] = known_names.astype(F32)
    wide[COL_FAR : COL_FAR + edges, :] = (names - owned - far * rim).astype(F32)
    for feature in range(features):
        wide[COL_EDGE + feature * edges : COL_EDGE + (feature + 1) * edges, :] = edge_ref[feature].astype(F32)
    table[...] = wide[...].T
    w_out[...] = jnp.zeros_like(w_out)
    w_out[0:fields, :] = w_out_ref[...]
    weights[...] = jnp.zeros_like(weights)
    weights[0:1, 0:fields] = weight_ref[...]
    known[owned + rim :, :] = jnp.zeros((LANES, channels), BF)
    for feature in range(features):
        half = (0.5 * w_edge_ref[feature : feature + 1, :].astype(F32)).astype(BF)
        for edge in range(edges):
            row = owned + rim + COL_EDGE + feature * edges + edge
            known[row : row + 1, :] = half
    loads[0].wait()
    loads[8].wait()
    zhat[...] = 0.5 * dot(grid_ref[...], w_dst_ref[...])
    to_near.wait_recv()

    def gather_known(part):
        rows = pl.ds(firsts[part], sizes[part])
        lane = lax.broadcasted_iota(jnp.int32, (sizes[part], LANES), 1)
        values = table[rows, :]
        hots = []
        for edge in range(edges):
            column = table[rows, COL_KNOWN + edge : COL_KNOWN + edge + 1].astype(jnp.int32)
            chosen = (lane >= COL_EDGE) & (lane < COL_FAR) & (lax.rem(lane, edges) == edge)
            hots.append(
                jnp.concatenate(
                    [
                        one_hot_columns(column, owned + rim),
                        jnp.where(chosen, values, 0.0).astype(BF),
                    ],
                    axis=1,
                )
            )
        found = dot(jnp.concatenate(hots, axis=0), known[...])
        dst = zhat[rows, :]
        for edge in range(edges):
            base[edge, rows, :] = found[edge * sizes[part] : (edge + 1) * sizes[part], :] + dst

    gather_known(0)
    gather_known(1)
    gather_known(2)
    loads[10].wait()

    gain = gain_ref[...]
    def read(part, side):
        rows = pl.ds(firsts[part], sizes[part])
        hots = [
            one_hot_columns(
                table[rows, COL_FAR + edge : COL_FAR + edge + 1].astype(jnp.int32) - side * (rim // 2),
                rim // 2,
            )
            for edge in range(edges)
        ]
        return dot(jnp.concatenate(hots, axis=0), away[halves[side], :])

    @pl.when(has_far)
    def _():
        to_far[0].wait_recv()

    for part in range(len(PARTS)):
        rows = pl.ds(firsts[part], sizes[part])
        found = read(part, 0)
        for edge in range(edges):
            base[edge, rows, :] += found[edge * sizes[part] : (edge + 1) * sizes[part], :]

    @pl.when(has_far)
    def _():
        to_far[1].wait_recv()

    def forward(part):
        rows = pl.ds(firsts[part], sizes[part])
        found = read(part, 1)
        total = None
        for edge in range(edges):
            half = found[edge * sizes[part] : (edge + 1) * sizes[part], :] + base[edge, rows, :]
            base[edge, rows, :] = half
            act = half * (jnp.tanh(half) + 1.0)
            total = act if total is None else total + act
        z = grid_ref[rows, :].astype(F32) + dot(total.astype(BF), w_msg_ref[...])
        centre = z - jnp.mean(z, axis=1, keepdims=True)
        scale = lax.rsqrt(jnp.mean(centre * centre, axis=1, keepdims=True) + LN_EPS)
        hat = centre * scale
        zhat[rows, :] = hat
        rstd[rows, :] = jnp.broadcast_to(scale, (sizes[part], LANES))
        pred[rows, :] = dot_t((hat * gain).astype(BF), w_out[...]).astype(BF)

    def derive(part):
        rows = pl.ds(firsts[part], sizes[part])
        total = None
        for edge in range(edges):
            half = base[edge, rows, :].astype(BF)
            rise = jnp.tanh(half) + 1.0
            twice = rise + half * rise * (2.0 - rise)
            deriv[edge, rows, :] = twice
            total = twice.astype(F32) if total is None else total + twice.astype(F32)
        deriv_sum[rows, :] = total

    def pred_copy(part, other):
        return remote(
            pred.at[pl.ds(firsts[part] + other * shares[part], shares[part])],
            peers.at[me, pl.ds(owns[part], shares[part])],
            pred_send,
            pred_recv.at[part],
            member=other,
        )

    def grad_copy(part, other):
        return remote(
            d_peers.at[other, pl.ds(owns[part], shares[part])],
            d_pred.at[pl.ds(firsts[part] + me * shares[part], shares[part])],
            d_send,
            d_recv.at[part],
            member=other,
        )

    def all_of(count, send_sem, recv_sem):
        size = pl.ds(0, count)
        return remote(pred.at[size], d_pred.at[size], send_sem, recv_sem, member=lax.rem(me + 1, n_member))

    def send_pred(part):
        for other in others():
            pred_copy(part, other).start()
        mine = pl.ds(pl.multiple_of(firsts[part] + me * shares[part], 16), shares[part])
        peers[me, pl.ds(owns[part], shares[part]), :] = pred[mine, :]

    def compare(part):
        all_of((n_member - 1) * shares[part], pred_send, pred_recv.at[part]).wait_recv()
        share = shares[part]
        rows = pl.ds(owns[part], share)
        mine = pl.ds(pl.multiple_of(firsts[part] + me * share, 16), share)
        goal = table[mine, :]
        lane = lax.broadcasted_iota(jnp.int32, (share, LANES), 1)
        goal = jnp.where(lane < fields, goal, 0.0)
        values = [peers[member, rows, :].astype(F32) for member in range(n_member)]
        spread = [jnp.zeros((share, LANES), F32) for _ in range(n_member)]
        for left in range(n_member):
            for right in range(left + 1, n_member):
                step = slope(values[left] - values[right])
                spread[left] = spread[left] + step
                spread[right] = spread[right] - step
        for member in range(n_member):
            grad = weights[...] * (slope(values[member] - goal) - coeff * spread[member])
            d_peers[member, rows, :] = grad.astype(BF)
        for other in others():
            grad_copy(part, other).start()
        d_pred[mine, :] = d_peers[me, rows, :]

    def backward(part):
        all_of((n_member - 1) * shares[part], d_send, d_recv.at[part]).wait_recv()
        rows = pl.ds(firsts[part], sizes[part])
        hat = zhat[rows, :]
        scale = rstd[rows, 0:1]
        scaled = dot(d_pred[rows, :], w_out[...]) * gain
        d_z = scale * (
            scaled
            - jnp.mean(scaled, axis=1, keepdims=True)
            - hat * jnp.mean(scaled * hat, axis=1, keepdims=True)
        )
        zhat[rows, :] = d_z
        d_act = 0.5 * dot_t(d_z.astype(BF), w_msg_ref[...])
        d_sum[rows, :] = (d_act * deriv_sum[rows, :]).astype(BF)
        d_act = d_act.astype(BF)
        for edge in range(edges):
            deriv[edge, rows, :] = d_act * deriv[edge, rows, :]

    def scatter(first_part, last_part, first, height):
        rows = pl.ds(firsts[first_part], firsts[last_part] + sizes[last_part] - firsts[first_part])
        names = jnp.concatenate([near_ref[edge : edge + 1, rows] for edge in range(edges)], axis=1)
        grads = jnp.concatenate([deriv[edge, rows, :] for edge in range(edges)], axis=0)
        return dot(one_hot_rows(names, height, first), grads)

    def scatter_far(part, first, count):
        return scatter(part, part, owned + far * rim + first, count)

    forward(0)
    send_pred(0)
    forward(1)
    send_pred(1)
    forward(2)
    send_pred(2)
    compare(0)
    derive(0)
    derive(1)
    compare(1)
    derive(2)
    compare(2)
    backward(0)
    rims[...] = scatter_far(0, 0, rim)
    backward(1)
    rims[...] += scatter_far(1, 0, rim)
    backward(2)
    back_near = remote(
        d_halo.at[0], back.at[pl.ds(0, rim)], back_send.at[0], back_recv.at[0], band=near_band
    )
    back_far = [
        remote(
            d_halo.at[1, rows],
            back.at[pl.ds(rim + i * (rim // 2), rim // 2)],
            back_send.at[1 + i],
            back_recv.at[1 + i],
            band=far_band,
        )
        for i, rows in enumerate(halves)
    ]
    d_halo[1, halves[0], :] = (rims[halves[0], :] + scatter_far(2, 0, rim // 2)).astype(BF)

    @pl.when(has_far)
    def _():
        back_far[0].start()

    d_halo[1, halves[1], :] = (rims[halves[1], :] + scatter_far(2, rim // 2, rim // 2)).astype(BF)

    @pl.when(has_far)
    def _():
        back_far[1].start()

    d_halo[0] = scatter(0, 2, owned + near * rim, rim).astype(BF)
    back_near.start()
    d_grid[...] = (zhat[...] + dot_t(d_sum[...], w_dst_ref[...])).astype(BF)
    slots[...] = scatter(0, 2, 0, owned)

    def returned(side, first, place, count):
        names = send_ref[pl.ds(side, 1), pl.ds(first, count)]
        return dot(one_hot_rows(names, owned, 0), back[pl.ds(place, count), :])

    back_near.wait_recv()
    slots[...] += returned(near, 0, 0, rim)

    @pl.when(has_far)
    def _():
        back_far[0].wait_recv()

    slots[...] += returned(far, 0, rim, rim // 2)

    @pl.when(has_far)
    def _():
        back_far[1].wait_recv()

    sums[...] = (slots[...] + returned(far, rim // 2, rim + rim // 2, rim // 2)).astype(BF)

    to_near.wait_send()
    back_near.wait_send()

    @pl.when(has_far)
    def _():
        for copy in to_far + back_far:
            copy.wait_send()

    all_of((n_member - 1) * sum(shares), pred_send, pred_recv.at[0]).wait_send()
    all_of((n_member - 1) * sum(shares), d_send, d_recv.at[0]).wait_send()


def finish(d_grid, sums, w_src, grid_out, mesh_out, rows_out, store_sem):
    through = pltpu.make_async_copy(d_grid, grid_out, store_sem.at[0])
    through.start()
    height = sums.shape[0] // 2
    stores = []
    for part in range(2):
        rows = pl.ds(part * height, height)
        rows_out[rows, :] = dot_t(sums[rows, :], w_src[...]).astype(BF)
        stores.append(
            pltpu.make_async_copy(rows_out.at[rows], mesh_out.at[rows], store_sem.at[part + 1])
        )
        stores[-1].start()
    through.wait()
    for store in stores:
        store.wait()


def per_device(
    n_band,
    n_member,
    grid_latent,
    mesh_latent,
    edge_attr,
    neighbours,
    send_rows,
    target,
    field_weight,
    w_src,
    w_dst,
    w_edge,
    w_msg,
    ln_gain,
    w_out,
):
    grid_rows = grid_latent[0]
    mesh_rows = mesh_latent[0]
    points, channels = grid_rows.shape
    owned = mesh_rows.shape[0]
    edges = neighbours.shape[1]
    rim = send_rows.shape[1]
    fields = target.shape[0]
    share = points // n_member
    operands = (
        grid_rows,
        mesh_rows,
        edge_attr,
        neighbours.T,
        send_rows,
        target,
        field_weight.reshape(1, fields),
        w_src,
        w_dst,
        w_edge,
        w_msg,
        ln_gain.reshape(1, channels),
        w_out.T,
    )
    anywhere = pl.BlockSpec(memory_space=pl.ANY)
    vmem = pl.BlockSpec(memory_space=pltpu.VMEM)
    dma = pltpu.SemaphoreType.DMA
    latents = pltpu.VMEM((points, channels), BF)
    wide_latents = pltpu.VMEM((points, channels), F32)
    d_grid, sums = pl.pallas_call(
        functools.partial(kernel, n_band, n_member),
        out_shape=(pltpu.VMEM((points, channels), BF), pltpu.VMEM((owned, channels), BF)),
        in_specs=[anywhere] * len(operands),
        out_specs=(vmem, vmem),
        scratch_shapes=[pltpu.VMEM(operand.shape, operand.dtype) for operand in operands]
        + [
            pltpu.VMEM((8, 2 * rim), F32),
            pltpu.VMEM((LANES, points), F32),
            pltpu.VMEM((points, LANES), F32),
            pltpu.VMEM((LANES, channels), BF),
            pltpu.VMEM((1, LANES), F32),
            pltpu.VMEM((2 * rim, 8), F32),
            pltpu.VMEM((owned + rim + LANES, channels), BF),
            pltpu.VMEM((2, rim, channels), BF),
            pltpu.VMEM((rim, channels), BF),
            pltpu.VMEM((edges, points, channels), F32),
            pltpu.VMEM((edges, points, channels), BF),
            wide_latents,
            wide_latents,
            pltpu.VMEM((points, LANES), F32),
            pltpu.VMEM((points, LANES), BF),
            pltpu.VMEM((n_member, share, LANES), BF),
            pltpu.VMEM((n_member, share, LANES), BF),
            pltpu.VMEM((points, LANES), BF),
            latents,
            wide_latents,
            pltpu.VMEM((rim, channels), F32),
            pltpu.VMEM((2, rim, channels), BF),
            pltpu.VMEM((2 * rim, channels), BF),
            dma((len(operands),)),
            dma((3,)),
            dma((3,)),
            dma,
            dma((len(PARTS),)),
            dma,
            dma((len(PARTS),)),
            dma((3,)),
            dma((3,)),
        ],
        compiler_params=pltpu.CompilerParams(
            collective_id=0, has_side_effects=True, vmem_limit_bytes=52 * 2**20
        ),
    )(*operands)
    d_grid, d_mesh = pl.pallas_call(
        finish,
        out_shape=(
            jax.ShapeDtypeStruct((points, channels), BF),
            jax.ShapeDtypeStruct((owned, channels), BF),
        ),
        in_specs=[vmem] * 3,
        out_specs=(anywhere, anywhere),
        scratch_shapes=[latents, dma((3,))],
        compiler_params=pltpu.CompilerParams(vmem_limit_bytes=16 * 2**20),
    )(d_grid, sums, w_src)
    return d_grid[None], d_mesh[None]


def solution(mesh):
    placed = (
        P("member", "band", None),
        P("member", "band", None),
        P(None, None, "band"),
        P("band", None),
        P("band", None),
        P(None, "band"),
        P(),
        P(),
        P(),
        P(),
        P(),
        P(),
        P(),
    )
    return jax.shard_map(
        functools.partial(per_device, mesh.shape["band"], mesh.shape["member"]),
        mesh=mesh,
        in_specs=placed,
        out_specs=(P("member", "band", None), P("member", "band", None)),
        check_vma=False,
    )
```

```python
import functools

import jax
import jax.numpy as jnp
from jax import lax
from jax.experimental import pallas as pl
from jax.experimental.pallas import tpu as pltpu
from jax.sharding import PartitionSpec as P

DELTA_SQ = 0.0625
ALPHA = 0.95
LN_EPS = 1e-05

BF = jnp.bfloat16
F32 = jnp.float32
LANES = 128
PARTS = (3, 3, 2)
UNIT = 128
MESH_ID = pl.DeviceIdType.MESH

COL_KNOWN = 100
COL_EDGE = 104
COL_FAR = 120


def dot(left, right):
    return jnp.dot(left, right, preferred_element_type=F32)


def dot_t(left, right):
    return lax.dot_general(left, right, (((1,), (1,)), ((), ())), preferred_element_type=F32)


def slope(diff):
    return diff * lax.rsqrt(diff * diff + DELTA_SQ)


def one_hot_columns(column, width):
    rows = column.shape[0]
    return jnp.where(lax.broadcasted_iota(jnp.int32, (rows, width), 1) == column, 1.0, 0.0).astype(BF)


def one_hot_rows(row, height, first):
    width = row.shape[1]
    return jnp.where(
        lax.broadcasted_iota(jnp.int32, (height, width), 0) + first == row, 1.0, 0.0
    ).astype(BF)


def remote(src, dst, send_sem, recv_sem, **where):
    return pltpu.make_async_remote_copy(
        src_ref=src, dst_ref=dst, send_sem=send_sem, recv_sem=recv_sem, device_id=where, device_id_type=MESH_ID
    )


def kernel(n_band, n_member, *refs):
    hbm, (d_grid, sums), refs = refs[:13], refs[13:15], refs[15:]
    held, refs = refs[:13], refs[13:]
    (
        grid_ref,
        mesh_ref,
        edge_ref,
        near_ref,
        send_ref,
        target_ref,
        weight_ref,
        w_src_ref,
        w_dst_ref,
        w_edge_ref,
        w_msg_ref,
        gain_ref,
        w_out_ref,
    ) = held
    (
        lists,
        wide,
        table,
        w_out,
        weights,
        columns,
        known,
        out_halo,
        away,
        base,
        found_far,
        deriv,
        zhat,
        rstd,
        pred,
        peers,
        d_peers,
        d_pred,
        d_halo,
        back,
        load_sem,
        halo_send,
        halo_recv,
        pred_send,
        pred_recv,
        d_send,
        d_recv,
        back_send,
        back_recv,
    ) = refs
    points, channels = grid_ref.shape
    owned = mesh_ref.shape[0]
    features = edge_ref.shape[0]
    edges = near_ref.shape[0]
    rim = send_ref.shape[1]
    fields = target_ref.shape[0]
    firsts = [sum(PARTS[:part]) * UNIT for part in range(len(PARTS))]
    sizes = [part * UNIT for part in PARTS]
    shares = [size // n_member for size in sizes]
    owns = [first // n_member for first in firsts]
    band = lax.axis_index("band")
    me = lax.axis_index("member")
    has_below = band > 0
    has_above = band < n_band - 1
    far = lax.rem(band, 2)
    near = 1 - far
    has_far = ((far == 0) & has_below) | ((far == 1) & has_above)
    near_band = band + 2 * near - 1
    far_band = jnp.clip(band + 2 * far - 1, 0, n_band - 1)
    coeff = ALPHA / (n_member - 1) + (1.0 - ALPHA) / n_member

    def others():
        ring = n_member // 2
        along, row = lax.rem(me, ring), me // ring
        hops = sorted(
            ((dy, dx) for dy in range(2) for dx in range(ring) if dy + dx > 0),
            key=lambda hop: -(hop[0] + min(hop[1], ring - hop[1])),
        )
        return [lax.rem(row + dy, 2) * ring + lax.rem(along + dx, ring) for dy, dx in hops]

    barrier = pltpu.get_barrier_semaphore()

    @pl.when(has_below)
    def _():
        pl.semaphore_signal(barrier, inc=1, device_id={"band": band - 1}, device_id_type=MESH_ID)

    @pl.when(has_above)
    def _():
        pl.semaphore_signal(barrier, inc=1, device_id={"band": band + 1}, device_id_type=MESH_ID)

    for other in others():
        pl.semaphore_signal(barrier, inc=1, device_id={"member": other}, device_id_type=MESH_ID)

    loads = [pltpu.make_async_copy(hbm[i], held[i], load_sem.at[i]) for i in range(13)]
    for i in (4, 7, 1):
        loads[i].start()

    loads[4].wait()
    lists[...] = jnp.zeros_like(lists)
    lists[0:1, 0:rim] = send_ref[0:1, :].astype(F32)
    lists[0:1, rim : 2 * rim] = send_ref[1:2, :].astype(F32)
    columns[...] = lists[...].T
    loads[7].wait()
    loads[1].wait()
    for i in (3, 2, 5, 9, 12, 6, 11, 0, 8, 10):
        loads[i].start()
    known[0:owned, :] = (0.5 * dot(mesh_ref[...], w_src_ref[...])).astype(BF)

    halves = (pl.ds(0, rim // 2), pl.ds(rim // 2, rim // 2))

    def select(side, first, count):
        rows = pl.ds(pl.multiple_of(side * rim + first, count), count)
        hot = one_hot_columns(columns[rows, 0:1].astype(jnp.int32), owned)
        return dot(hot, known[0:owned, :]).astype(BF)

    to_near = remote(
        out_halo.at[0], known.at[pl.ds(owned, rim)], halo_send.at[0], halo_recv.at[0], band=near_band
    )
    to_far = [
        remote(
            out_halo.at[1, rows], away.at[rows], halo_send.at[1 + i], halo_recv.at[1 + i], band=far_band
        )
        for i, rows in enumerate(halves)
    ]
    out_halo[1, halves[0], :] = select(far, 0, rim // 2)
    pl.semaphore_wait(
        barrier, n_member - 1 + jnp.where(has_below, 1, 0) + jnp.where(has_above, 1, 0)
    )

    @pl.when(has_far)
    def _():
        to_far[0].start()

    out_halo[1, halves[1], :] = select(far, rim // 2, rim // 2)

    @pl.when(has_far)
    def _():
        to_far[1].start()

    out_halo[0] = select(near, 0, rim)
    to_near.start()

    @pl.when(jnp.logical_not(has_far))
    def _():
        away[0:rim, :] = jnp.zeros((rim, channels), BF)
        back[rim : 2 * rim, :] = jnp.zeros((rim, channels), BF)

    for i in (3, 2, 5, 9, 12, 6, 11):
        loads[i].wait()
    names = near_ref[...]
    in_near = (names >= owned + near * rim) & (names < owned + (near + 1) * rim)
    known_names = jnp.where(in_near, names - near * rim, jnp.where(names < owned, names, -1))
    wide[...] = jnp.zeros_like(wide)
    wide[0:fields, :] = target_ref[...]
    wide[COL_KNOWN : COL_KNOWN + edges, :] = known_names.astype(F32)
    wide[COL_FAR : COL_FAR + edges, :] = (names - owned - far * rim).astype(F32)
    for feature in range(features):
        wide[COL_EDGE + feature * edges : COL_EDGE + (feature + 1) * edges, :] = edge_ref[feature].astype(F32)
    table[...] = wide[...].T
    w_out[...] = jnp.zeros_like(w_out)
    w_out[0:fields, :] = w_out_ref[...]
    weights[...] = jnp.zeros_like(weights)
    weights[0:1, 0:fields] = weight_ref[...]
    known[owned + rim :, :] = jnp.zeros((LANES, channels), BF)
    for feature in range(features):
        half = (0.5 * w_edge_ref[feature : feature + 1, :].astype(F32)).astype(BF)
        for edge in range(edges):
            row = owned + rim + COL_EDGE + feature * edges + edge
            known[row : row + 1, :] = half
    loads[0].wait()
    loads[8].wait()
    zhat[...] = 0.5 * dot(grid_ref[...], w_dst_ref[...])
    to_near.wait_recv()

    def gather_known(part):
        rows = pl.ds(firsts[part], sizes[part])
        lane = lax.broadcasted_iota(jnp.int32, (sizes[part], LANES), 1)
        values = table[rows, :]
        hots = []
        for edge in range(edges):
            column = table[rows, COL_KNOWN + edge : COL_KNOWN + edge + 1].astype(jnp.int32)
            chosen = (lane >= COL_EDGE) & (lane < COL_FAR) & (lax.rem(lane, edges) == edge)
            hots.append(
                jnp.concatenate(
                    [
                        one_hot_columns(column, owned + rim),
                        jnp.where(chosen, values, 0.0).astype(BF),
                    ],
                    axis=1,
                )
            )
        found = dot(jnp.concatenate(hots, axis=0), known[...])
        dst = zhat[rows, :]
        for edge in range(edges):
            base[edge, rows, :] = found[edge * sizes[part] : (edge + 1) * sizes[part], :] + dst

    gather_known(0)
    gather_known(1)
    gather_known(2)
    loads[10].wait()

    @pl.when(has_far)
    def _():
        to_far[0].wait_recv()
        to_far[1].wait_recv()

    gain = gain_ref[...]

    def read(part):
        rows = pl.ds(firsts[part], sizes[part])
        hots = [
            one_hot_columns(table[rows, COL_FAR + edge : COL_FAR + edge + 1].astype(jnp.int32), rim)
            for edge in range(edges)
        ]
        found = dot(jnp.concatenate(hots, axis=0), away[...])
        found_far[0 : edges * sizes[part], :] = found

    def forward(part):
        rows = pl.ds(firsts[part], sizes[part])
        total = None
        for edge in range(edges):
            half = found_far[edge * sizes[part] : (edge + 1) * sizes[part], :] + base[edge, rows, :]
            base[edge, rows, :] = half
            act = half * (jnp.tanh(half) + 1.0)
            total = act if total is None else total + act
        z = grid_ref[rows, :].astype(F32) + dot(total.astype(BF), w_msg_ref[...])
        centre = z - jnp.mean(z, axis=1, keepdims=True)
        scale = lax.rsqrt(jnp.mean(centre * centre, axis=1, keepdims=True) + LN_EPS)
        hat = centre * scale
        zhat[rows, :] = hat
        rstd[rows, :] = jnp.broadcast_to(scale, (sizes[part], LANES))
        pred[rows, :] = dot_t((hat * gain).astype(BF), w_out[...]).astype(BF)

    def derive(part):
        rows = pl.ds(firsts[part], sizes[part])
        for edge in range(edges):
            half = base[edge, rows, :].astype(BF)
            rise = jnp.tanh(half) + 1.0
            twice = rise + half * rise * (2.0 - rise)
            deriv[edge, rows, :] = twice

    def pred_copy(part, other):
        return remote(
            pred.at[pl.ds(firsts[part] + other * shares[part], shares[part])],
            peers.at[me, pl.ds(owns[part], shares[part])],
            pred_send,
            pred_recv.at[part],
            member=other,
        )

    def grad_copy(part, other):
        return remote(
            d_peers.at[other, pl.ds(owns[part], shares[part])],
            d_pred.at[pl.ds(firsts[part] + me * shares[part], shares[part])],
            d_send,
            d_recv.at[part],
            member=other,
        )

    def all_of(count, send_sem, recv_sem):
        size = pl.ds(0, count)
        return remote(pred.at[size], d_pred.at[size], send_sem, recv_sem, member=lax.rem(me + 1, n_member))

    def send_pred(part):
        for other in others():
            pred_copy(part, other).start()
        mine = pl.ds(pl.multiple_of(firsts[part] + me * shares[part], 16), shares[part])
        peers[me, pl.ds(owns[part], shares[part]), :] = pred[mine, :]

    def compare(part):
        all_of((n_member - 1) * shares[part], pred_send, pred_recv.at[part]).wait_recv()
        share = shares[part]
        rows = pl.ds(owns[part], share)
        mine = pl.ds(pl.multiple_of(firsts[part] + me * share, 16), share)
        goal = table[mine, :]
        lane = lax.broadcasted_iota(jnp.int32, (share, LANES), 1)
        goal = jnp.where(lane < fields, goal, 0.0)
        values = [peers[member, rows, :].astype(F32) for member in range(n_member)]
        spread = [jnp.zeros((share, LANES), F32) for _ in range(n_member)]
        for left in range(n_member):
            for right in range(left + 1, n_member):
                step = slope(values[left] - values[right])
                spread[left] = spread[left] + step
                spread[right] = spread[right] - step
        for member in range(n_member):
            grad = weights[...] * (slope(values[member] - goal) - coeff * spread[member])
            d_peers[member, rows, :] = grad.astype(BF)
        for other in others():
            grad_copy(part, other).start()
        d_pred[mine, :] = d_peers[me, rows, :]

    def backward(part):
        all_of((n_member - 1) * shares[part], d_send, d_recv.at[part]).wait_recv()
        rows = pl.ds(firsts[part], sizes[part])
        hat = zhat[rows, :]
        scale = rstd[rows, 0:1]
        scaled = dot(d_pred[rows, :], w_out[...]) * gain
        d_z = scale * (
            scaled
            - jnp.mean(scaled, axis=1, keepdims=True)
            - hat * jnp.mean(scaled * hat, axis=1, keepdims=True)
        )
        zhat[rows, :] = d_z
        d_act = (0.5 * dot_t(d_z.astype(BF), w_msg_ref[...])).astype(BF)
        for edge in range(edges):
            deriv[edge, rows, :] = d_act * deriv[edge, rows, :]

    def scatter(first_part, last_part, first, height):
        rows = pl.ds(firsts[first_part], firsts[last_part] + sizes[last_part] - firsts[first_part])
        names = jnp.concatenate([near_ref[edge : edge + 1, rows] for edge in range(edges)], axis=1)
        grads = jnp.concatenate([deriv[edge, rows, :] for edge in range(edges)], axis=0)
        return dot(one_hot_rows(names, height, first), grads)

    slots, rims = base.at[0], base.at[1, pl.ds(0, rim)]

    def scatter_far(part, first, count):
        return scatter(part, part, owned + far * rim + first, count)

    read(0)
    forward(0)
    send_pred(0)
    read(1)
    forward(1)
    send_pred(1)
    read(2)
    forward(2)
    send_pred(2)
    compare(0)
    derive(0)
    compare(1)
    derive(1)
    derive(2)
    compare(2)
    backward(0)
    rims[...] = scatter_far(0, 0, rim)
    backward(1)
    rims[...] += scatter_far(1, 0, rim)
    backward(2)
    back_near = remote(
        d_halo.at[0], back.at[pl.ds(0, rim)], back_send.at[0], back_recv.at[0], band=near_band
    )
    back_far = [
        remote(
            d_halo.at[1, rows],
            back.at[pl.ds(rim + i * (rim // 2), rim // 2)],
            back_send.at[1 + i],
            back_recv.at[1 + i],
            band=far_band,
        )
        for i, rows in enumerate(halves)
    ]
    d_halo[1, halves[0], :] = (rims[halves[0], :] + scatter_far(2, 0, rim // 2)).astype(BF)

    @pl.when(has_far)
    def _():
        back_far[0].start()

    d_halo[1, halves[1], :] = (rims[halves[1], :] + scatter_far(2, rim // 2, rim // 2)).astype(BF)

    @pl.when(has_far)
    def _():
        back_far[1].start()

    d_halo[0] = scatter(0, 2, owned + near * rim, rim).astype(BF)
    back_near.start()
    d_sum = deriv[0].astype(F32)
    for edge in range(1, edges):
        d_sum = d_sum + deriv[edge].astype(F32)
    d_grid[...] = (zhat[...] + dot_t(d_sum.astype(BF), w_dst_ref[...])).astype(BF)
    slots[...] = scatter(0, 2, 0, owned)

    def returned(side, first, place, count):
        names = send_ref[pl.ds(side, 1), pl.ds(first, count)]
        return dot(one_hot_rows(names, owned, 0), back[pl.ds(place, count), :])

    back_near.wait_recv()
    slots[...] += returned(near, 0, 0, rim)

    @pl.when(has_far)
    def _():
        back_far[0].wait_recv()

    slots[...] += returned(far, 0, rim, rim // 2)

    @pl.when(has_far)
    def _():
        back_far[1].wait_recv()

    sums[...] = (slots[...] + returned(far, rim // 2, rim + rim // 2, rim // 2)).astype(BF)

    to_near.wait_send()
    back_near.wait_send()

    @pl.when(has_far)
    def _():
        for copy in to_far + back_far:
            copy.wait_send()

    all_of((n_member - 1) * sum(shares), pred_send, pred_recv.at[0]).wait_send()
    all_of((n_member - 1) * sum(shares), d_send, d_recv.at[0]).wait_send()


def finish(d_grid, sums, w_src, grid_out, mesh_out, rows_out, store_sem):
    through = pltpu.make_async_copy(d_grid, grid_out, store_sem.at[0])
    through.start()
    height = sums.shape[0] // 4
    stores = []
    for part in range(4):
        rows = pl.ds(part * height, height)
        rows_out[rows, :] = dot_t(sums[rows, :], w_src[...]).astype(BF)
        stores.append(
            pltpu.make_async_copy(rows_out.at[rows], mesh_out.at[rows], store_sem.at[part + 1])
        )
        stores[-1].start()
    through.wait()
    for store in stores:
        store.wait()


def per_device(
    n_band,
    n_member,
    grid_latent,
    mesh_latent,
    edge_attr,
    neighbours,
    send_rows,
    target,
    field_weight,
    w_src,
    w_dst,
    w_edge,
    w_msg,
    ln_gain,
    w_out,
):
    grid_rows = grid_latent[0]
    mesh_rows = mesh_latent[0]
    points, channels = grid_rows.shape
    owned = mesh_rows.shape[0]
    edges = neighbours.shape[1]
    rim = send_rows.shape[1]
    fields = target.shape[0]
    share = points // n_member
    largest = max(PARTS) * UNIT
    operands = (
        grid_rows,
        mesh_rows,
        edge_attr,
        neighbours.T,
        send_rows,
        target,
        field_weight.reshape(1, fields),
        w_src,
        w_dst,
        w_edge,
        w_msg,
        ln_gain.reshape(1, channels),
        w_out.T,
    )
    anywhere = pl.BlockSpec(memory_space=pl.ANY)
    vmem = pl.BlockSpec(memory_space=pltpu.VMEM)
    dma = pltpu.SemaphoreType.DMA
    latents = pltpu.VMEM((points, channels), BF)
    wide_latents = pltpu.VMEM((points, channels), F32)
    d_grid, sums = pl.pallas_call(
        functools.partial(kernel, n_band, n_member),
        out_shape=(pltpu.VMEM((points, channels), BF), pltpu.VMEM((owned, channels), BF)),
        in_specs=[anywhere] * len(operands),
        out_specs=(vmem, vmem),
        scratch_shapes=[pltpu.VMEM(operand.shape, operand.dtype) for operand in operands]
        + [
            pltpu.VMEM((8, 2 * rim), F32),
            pltpu.VMEM((LANES, points), F32),
            pltpu.VMEM((points, LANES), F32),
            pltpu.VMEM((LANES, channels), BF),
            pltpu.VMEM((1, LANES), F32),
            pltpu.VMEM((2 * rim, 8), F32),
            pltpu.VMEM((owned + rim + LANES, channels), BF),
            pltpu.VMEM((2, rim, channels), BF),
            pltpu.VMEM((rim, channels), BF),
            pltpu.VMEM((edges, points, channels), F32),
            pltpu.VMEM((edges * largest, channels), F32),
            pltpu.VMEM((edges, points, channels), BF),
            wide_latents,
            pltpu.VMEM((points, LANES), F32),
            pltpu.VMEM((points, LANES), BF),
            pltpu.VMEM((n_member, share, LANES), BF),
            pltpu.VMEM((n_member, share, LANES), BF),
            pltpu.VMEM((points, LANES), BF),
            pltpu.VMEM((2, rim, channels), BF),
            pltpu.VMEM((2 * rim, channels), BF),
            dma((len(operands),)),
            dma((3,)),
            dma((3,)),
            dma,
            dma((len(PARTS),)),
            dma,
            dma((len(PARTS),)),
            dma((3,)),
            dma((3,)),
        ],
        compiler_params=pltpu.CompilerParams(
            collective_id=0, has_side_effects=True, vmem_limit_bytes=52 * 2**20
        ),
    )(*operands)
    d_grid, d_mesh = pl.pallas_call(
        finish,
        out_shape=(
            jax.ShapeDtypeStruct((points, channels), BF),
            jax.ShapeDtypeStruct((owned, channels), BF),
        ),
        in_specs=[vmem] * 3,
        out_specs=(anywhere, anywhere),
        scratch_shapes=[latents, dma((5,))],
        compiler_params=pltpu.CompilerParams(vmem_limit_bytes=16 * 2**20),
    )(d_grid, sums, w_src)
    return d_grid[None], d_mesh[None]


def solution(mesh):
    placed = (
        P("member", "band", None),
        P("member", "band", None),
        P(None, None, "band"),
        P("band", None),
        P("band", None),
        P(None, "band"),
        P(),
        P(),
        P(),
        P(),
        P(),
        P(),
        P(),
    )
    return jax.shard_map(
        functools.partial(per_device, mesh.shape["band"], mesh.shape["member"]),
        mesh=mesh,
        in_specs=placed,
        out_specs=(P("member", "band", None), P("member", "band", None)),
        check_vma=False,
    )
```

```python
import functools

import jax
import jax.numpy as jnp
from jax import lax
from jax.experimental import pallas as pl
from jax.experimental.pallas import tpu as pltpu
from jax.sharding import PartitionSpec as P

DELTA_SQ = 0.0625
ALPHA = 0.95
LN_EPS = 1e-05

BF = jnp.bfloat16
F32 = jnp.float32
LANES = 128
PARTS = (3, 3, 2)
UNIT = 128
MESH_ID = pl.DeviceIdType.MESH

COL_KNOWN = 100
COL_EDGE = 104
COL_FAR = 120


def dot(left, right):
    return jnp.dot(left, right, preferred_element_type=F32)


def dot_t(left, right):
    return lax.dot_general(left, right, (((1,), (1,)), ((), ())), preferred_element_type=F32)


def slope(diff):
    return diff * lax.rsqrt(diff * diff + DELTA_SQ)


def one_hot_columns(column, width):
    rows = column.shape[0]
    return jnp.where(lax.broadcasted_iota(jnp.int32, (rows, width), 1) == column, 1.0, 0.0).astype(BF)


def one_hot_rows(row, height, first):
    width = row.shape[1]
    return jnp.where(
        lax.broadcasted_iota(jnp.int32, (height, width), 0) + first == row, 1.0, 0.0
    ).astype(BF)


def remote(src, dst, send_sem, recv_sem, **where):
    return pltpu.make_async_remote_copy(
        src_ref=src, dst_ref=dst, send_sem=send_sem, recv_sem=recv_sem, device_id=where, device_id_type=MESH_ID
    )


def kernel(n_band, n_member, *refs):
    hbm, (d_grid, sums), refs = refs[:13], refs[13:15], refs[15:]
    held, refs = refs[:13], refs[13:]
    (
        grid_ref,
        mesh_ref,
        edge_ref,
        near_ref,
        send_ref,
        target_ref,
        weight_ref,
        w_src_ref,
        w_dst_ref,
        w_edge_ref,
        w_msg_ref,
        gain_ref,
        w_out_ref,
    ) = held
    (
        lists,
        wide,
        table,
        w_out,
        weights,
        columns,
        known,
        out_halo,
        away,
        base,
        found_far,
        deriv,
        zhat,
        rstd,
        pred,
        peers,
        d_peers,
        d_pred,
        d_halo,
        back,
        load_sem,
        halo_send,
        halo_recv,
        pred_send,
        pred_recv,
        d_send,
        d_recv,
        back_send,
        back_recv,
    ) = refs
    points, channels = grid_ref.shape
    owned = mesh_ref.shape[0]
    features = edge_ref.shape[0]
    edges = near_ref.shape[0]
    rim = send_ref.shape[1]
    fields = target_ref.shape[0]
    firsts = [sum(PARTS[:part]) * UNIT for part in range(len(PARTS))]
    sizes = [part * UNIT for part in PARTS]
    shares = [size // n_member for size in sizes]
    owns = [first // n_member for first in firsts]
    band = lax.axis_index("band")
    me = lax.axis_index("member")
    has_below = band > 0
    has_above = band < n_band - 1
    far = lax.rem(band, 2)
    near = 1 - far
    has_far = ((far == 0) & has_below) | ((far == 1) & has_above)
    near_band = band + 2 * near - 1
    far_band = jnp.clip(band + 2 * far - 1, 0, n_band - 1)
    coeff = ALPHA / (n_member - 1) + (1.0 - ALPHA) / n_member

    def others():
        ring = n_member // 2
        along, row = lax.rem(me, ring), me // ring
        hops = sorted(
            ((dy, dx) for dy in range(2) for dx in range(ring) if dy + dx > 0),
            key=lambda hop: -(hop[0] + min(hop[1], ring - hop[1])),
        )
        return [lax.rem(row + dy, 2) * ring + lax.rem(along + dx, ring) for dy, dx in hops]

    barrier = pltpu.get_barrier_semaphore()

    @pl.when(has_below)
    def _():
        pl.semaphore_signal(barrier, inc=1, device_id={"band": band - 1}, device_id_type=MESH_ID)

    @pl.when(has_above)
    def _():
        pl.semaphore_signal(barrier, inc=1, device_id={"band": band + 1}, device_id_type=MESH_ID)

    for other in others():
        pl.semaphore_signal(barrier, inc=1, device_id={"member": other}, device_id_type=MESH_ID)

    loads = [pltpu.make_async_copy(hbm[i], held[i], load_sem.at[i]) for i in range(13)]
    for i in (4, 7, 1):
        loads[i].start()

    loads[4].wait()
    lists[...] = jnp.zeros_like(lists)
    lists[0:1, 0:rim] = send_ref[0:1, :].astype(F32)
    lists[0:1, rim : 2 * rim] = send_ref[1:2, :].astype(F32)
    columns[...] = lists[...].T
    loads[7].wait()
    loads[1].wait()
    for i in (3, 2, 5, 9, 12, 6, 11, 0, 8, 10):
        loads[i].start()
    known[0:owned, :] = (0.5 * dot(mesh_ref[...], w_src_ref[...])).astype(BF)

    halves = (pl.ds(0, rim // 2), pl.ds(rim // 2, rim // 2))

    def select(side, first, count):
        rows = pl.ds(pl.multiple_of(side * rim + first, count), count)
        hot = one_hot_columns(columns[rows, 0:1].astype(jnp.int32), owned)
        return dot(hot, known[0:owned, :]).astype(BF)

    to_near = remote(
        out_halo.at[0], known.at[pl.ds(owned, rim)], halo_send.at[0], halo_recv.at[0], band=near_band
    )
    to_far = [
        remote(
            out_halo.at[1, rows], away.at[rows], halo_send.at[1 + i], halo_recv.at[1 + i], band=far_band
        )
        for i, rows in enumerate(halves)
    ]
    out_halo[1, halves[0], :] = select(far, 0, rim // 2)
    pl.semaphore_wait(
        barrier, n_member - 1 + jnp.where(has_below, 1, 0) + jnp.where(has_above, 1, 0)
    )

    @pl.when(has_far)
    def _():
        to_far[0].start()

    out_halo[0] = select(near, 0, rim)
    to_near.start()
    out_halo[1, halves[1], :] = select(far, rim // 2, rim // 2)

    @pl.when(has_far)
    def _():
        to_far[1].start()

    @pl.when(jnp.logical_not(has_far))
    def _():
        away[0:rim, :] = jnp.zeros((rim, channels), BF)
        back[rim : 2 * rim, :] = jnp.zeros((rim, channels), BF)

    for i in (3, 2, 5, 9, 12, 6, 11):
        loads[i].wait()
    names = near_ref[...]
    in_near = (names >= owned + near * rim) & (names < owned + (near + 1) * rim)
    known_names = jnp.where(in_near, names - near * rim, jnp.where(names < owned, names, -1))
    wide[...] = jnp.zeros_like(wide)
    wide[0:fields, :] = target_ref[...]
    wide[COL_KNOWN : COL_KNOWN + edges, :] = known_names.astype(F32)
    wide[COL_FAR : COL_FAR + edges, :] = (names - owned - far * rim).astype(F32)
    for feature in range(features):
        wide[COL_EDGE + feature * edges : COL_EDGE + (feature + 1) * edges, :] = edge_ref[feature].astype(F32)
    table[...] = wide[...].T
    w_out[...] = jnp.zeros_like(w_out)
    w_out[0:fields, :] = w_out_ref[...]
    weights[...] = jnp.zeros_like(weights)
    weights[0:1, 0:fields] = weight_ref[...]
    known[owned + rim :, :] = jnp.zeros((LANES, channels), BF)
    for feature in range(features):
        half = (0.5 * w_edge_ref[feature : feature + 1, :].astype(F32)).astype(BF)
        for edge in range(edges):
            row = owned + rim + COL_EDGE + feature * edges + edge
            known[row : row + 1, :] = half
    loads[0].wait()
    loads[8].wait()
    zhat[...] = 0.5 * dot(grid_ref[...], w_dst_ref[...])
    to_near.wait_recv()

    def gather_known(part):
        rows = pl.ds(firsts[part], sizes[part])
        lane = lax.broadcasted_iota(jnp.int32, (sizes[part], LANES), 1)
        values = table[rows, :]
        hots = []
        for edge in range(edges):
            column = table[rows, COL_KNOWN + edge : COL_KNOWN + edge + 1].astype(jnp.int32)
            chosen = (lane >= COL_EDGE) & (lane < COL_FAR) & (lax.rem(lane, edges) == edge)
            hots.append(
                jnp.concatenate(
                    [
                        one_hot_columns(column, owned + rim),
                        jnp.where(chosen, values, 0.0).astype(BF),
                    ],
                    axis=1,
                )
            )
        found = dot(jnp.concatenate(hots, axis=0), known[...])
        dst = zhat[rows, :]
        for edge in range(edges):
            base[edge, rows, :] = found[edge * sizes[part] : (edge + 1) * sizes[part], :] + dst

    gather_known(0)
    gather_known(1)
    gather_known(2)
    loads[10].wait()

    @pl.when(has_far)
    def _():
        to_far[0].wait_recv()
        to_far[1].wait_recv()

    gain = gain_ref[...]

    def read(part):
        rows = pl.ds(firsts[part], sizes[part])
        hots = [
            one_hot_columns(table[rows, COL_FAR + edge : COL_FAR + edge + 1].astype(jnp.int32), rim)
            for edge in range(edges)
        ]
        found = dot(jnp.concatenate(hots, axis=0), away[...])
        found_far[0 : edges * sizes[part], :] = found

    def forward(part):
        rows = pl.ds(firsts[part], sizes[part])
        total = None
        for edge in range(edges):
            half = found_far[edge * sizes[part] : (edge + 1) * sizes[part], :] + base[edge, rows, :]
            base[edge, rows, :] = half
            act = half * (jnp.tanh(half) + 1.0)
            total = act if total is None else total + act
        z = grid_ref[rows, :].astype(F32) + dot(total.astype(BF), w_msg_ref[...])
        centre = z - jnp.mean(z, axis=1, keepdims=True)
        scale = lax.rsqrt(jnp.mean(centre * centre, axis=1, keepdims=True) + LN_EPS)
        hat = centre * scale
        zhat[rows, :] = hat
        rstd[rows, :] = jnp.broadcast_to(scale, (sizes[part], LANES))
        pred[rows, :] = dot_t((hat * gain).astype(BF), w_out[...]).astype(BF)

    def derive(part):
        rows = pl.ds(firsts[part], sizes[part])
        for edge in range(edges):
            half = base[edge, rows, :].astype(BF)
            rise = jnp.tanh(half) + 1.0
            twice = rise + half * rise * (2.0 - rise)
            deriv[edge, rows, :] = twice

    def pred_copy(part, other):
        return remote(
            pred.at[pl.ds(firsts[part] + other * shares[part], shares[part])],
            peers.at[me, pl.ds(owns[part], shares[part])],
            pred_send,
            pred_recv.at[part],
            member=other,
        )

    def grad_copy(part, other):
        return remote(
            d_peers.at[other, pl.ds(owns[part], shares[part])],
            d_pred.at[pl.ds(firsts[part] + me * shares[part], shares[part])],
            d_send,
            d_recv.at[part],
            member=other,
        )

    def all_of(count, send_sem, recv_sem):
        size = pl.ds(0, count)
        return remote(pred.at[size], d_pred.at[size], send_sem, recv_sem, member=lax.rem(me + 1, n_member))

    def send_pred(part):
        for other in others():
            pred_copy(part, other).start()
        mine = pl.ds(pl.multiple_of(firsts[part] + me * shares[part], 16), shares[part])
        peers[me, pl.ds(owns[part], shares[part]), :] = pred[mine, :]

    def compare(part):
        all_of((n_member - 1) * shares[part], pred_send, pred_recv.at[part]).wait_recv()
        share = shares[part]
        rows = pl.ds(owns[part], share)
        mine = pl.ds(pl.multiple_of(firsts[part] + me * share, 16), share)
        goal = table[mine, :]
        lane = lax.broadcasted_iota(jnp.int32, (share, LANES), 1)
        goal = jnp.where(lane < fields, goal, 0.0)
        values = [peers[member, rows, :].astype(F32) for member in range(n_member)]
        spread = [jnp.zeros((share, LANES), F32) for _ in range(n_member)]
        for left in range(n_member):
            for right in range(left + 1, n_member):
                step = slope(values[left] - values[right])
                spread[left] = spread[left] + step
                spread[right] = spread[right] - step
        for member in range(n_member):
            grad = weights[...] * (slope(values[member] - goal) - coeff * spread[member])
            d_peers[member, rows, :] = grad.astype(BF)
        for other in others():
            grad_copy(part, other).start()
        d_pred[mine, :] = d_peers[me, rows, :]

    def backward(part):
        all_of((n_member - 1) * shares[part], d_send, d_recv.at[part]).wait_recv()
        rows = pl.ds(firsts[part], sizes[part])
        hat = zhat[rows, :]
        scale = rstd[rows, 0:1]
        scaled = dot(d_pred[rows, :], w_out[...]) * gain
        d_z = scale * (
            scaled
            - jnp.mean(scaled, axis=1, keepdims=True)
            - hat * jnp.mean(scaled * hat, axis=1, keepdims=True)
        )
        zhat[rows, :] = d_z
        d_act = (0.5 * dot_t(d_z.astype(BF), w_msg_ref[...])).astype(BF)
        for edge in range(edges):
            deriv[edge, rows, :] = d_act * deriv[edge, rows, :]

    def scatter(first_part, last_part, first, height):
        rows = pl.ds(firsts[first_part], firsts[last_part] + sizes[last_part] - firsts[first_part])
        names = jnp.concatenate([near_ref[edge : edge + 1, rows] for edge in range(edges)], axis=1)
        grads = jnp.concatenate([deriv[edge, rows, :] for edge in range(edges)], axis=0)
        return dot(one_hot_rows(names, height, first), grads)

    slots, rims = base.at[0], base.at[1, pl.ds(0, rim)]

    def scatter_far(part, first, count):
        return scatter(part, part, owned + far * rim + first, count)

    read(0)
    forward(0)
    send_pred(0)
    read(1)
    forward(1)
    send_pred(1)
    read(2)
    forward(2)
    send_pred(2)
    compare(0)
    derive(0)
    compare(1)
    derive(1)
    derive(2)
    compare(2)
    backward(0)
    rims[...] = scatter_far(0, 0, rim)
    backward(1)
    rims[...] += scatter_far(1, 0, rim)
    backward(2)
    back_near = remote(
        d_halo.at[0], back.at[pl.ds(0, rim)], back_send.at[0], back_recv.at[0], band=near_band
    )
    back_far = [
        remote(
            d_halo.at[1, rows],
            back.at[pl.ds(rim + i * (rim // 2), rim // 2)],
            back_send.at[1 + i],
            back_recv.at[1 + i],
            band=far_band,
        )
        for i, rows in enumerate(halves)
    ]
    d_halo[1, halves[0], :] = (rims[halves[0], :] + scatter_far(2, 0, rim // 2)).astype(BF)

    @pl.when(has_far)
    def _():
        back_far[0].start()

    d_halo[1, halves[1], :] = (rims[halves[1], :] + scatter_far(2, rim // 2, rim // 2)).astype(BF)

    @pl.when(has_far)
    def _():
        back_far[1].start()

    d_halo[0] = scatter(0, 2, owned + near * rim, rim).astype(BF)
    back_near.start()
    d_sum = deriv[0].astype(F32)
    for edge in range(1, edges):
        d_sum = d_sum + deriv[edge].astype(F32)
    d_grid[...] = (zhat[...] + dot_t(d_sum.astype(BF), w_dst_ref[...])).astype(BF)
    slots[...] = scatter(0, 2, 0, owned)

    def returned(side, first, place, count):
        names = send_ref[pl.ds(side, 1), pl.ds(first, count)]
        return dot(one_hot_rows(names, owned, 0), back[pl.ds(place, count), :])

    back_near.wait_recv()
    slots[...] += returned(near, 0, 0, rim)

    @pl.when(has_far)
    def _():
        back_far[0].wait_recv()

    slots[...] += returned(far, 0, rim, rim // 2)

    @pl.when(has_far)
    def _():
        back_far[1].wait_recv()

    sums[...] = (slots[...] + returned(far, rim // 2, rim + rim // 2, rim // 2)).astype(BF)

    to_near.wait_send()
    back_near.wait_send()

    @pl.when(has_far)
    def _():
        for copy in to_far + back_far:
            copy.wait_send()

    all_of((n_member - 1) * sum(shares), pred_send, pred_recv.at[0]).wait_send()
    all_of((n_member - 1) * sum(shares), d_send, d_recv.at[0]).wait_send()


def finish(d_grid, sums, w_src, grid_out, mesh_out, rows_out, store_sem):
    through = pltpu.make_async_copy(d_grid, grid_out, store_sem.at[0])
    through.start()
    height = sums.shape[0] // 4
    stores = []
    for part in range(4):
        rows = pl.ds(part * height, height)
        rows_out[rows, :] = dot_t(sums[rows, :], w_src[...]).astype(BF)
        stores.append(
            pltpu.make_async_copy(rows_out.at[rows], mesh_out.at[rows], store_sem.at[part + 1])
        )
        stores[-1].start()
    through.wait()
    for store in stores:
        store.wait()


def per_device(
    n_band,
    n_member,
    grid_latent,
    mesh_latent,
    edge_attr,
    neighbours,
    send_rows,
    target,
    field_weight,
    w_src,
    w_dst,
    w_edge,
    w_msg,
    ln_gain,
    w_out,
):
    grid_rows = grid_latent[0]
    mesh_rows = mesh_latent[0]
    points, channels = grid_rows.shape
    owned = mesh_rows.shape[0]
    edges = neighbours.shape[1]
    rim = send_rows.shape[1]
    fields = target.shape[0]
    share = points // n_member
    largest = max(PARTS) * UNIT
    operands = (
        grid_rows,
        mesh_rows,
        edge_attr,
        neighbours.T,
        send_rows,
        target,
        field_weight.reshape(1, fields),
        w_src,
        w_dst,
        w_edge,
        w_msg,
        ln_gain.reshape(1, channels),
        w_out.T,
    )
    anywhere = pl.BlockSpec(memory_space=pl.ANY)
    vmem = pl.BlockSpec(memory_space=pltpu.VMEM)
    dma = pltpu.SemaphoreType.DMA
    latents = pltpu.VMEM((points, channels), BF)
    wide_latents = pltpu.VMEM((points, channels), F32)
    d_grid, sums = pl.pallas_call(
        functools.partial(kernel, n_band, n_member),
        out_shape=(pltpu.VMEM((points, channels), BF), pltpu.VMEM((owned, channels), BF)),
        in_specs=[anywhere] * len(operands),
        out_specs=(vmem, vmem),
        scratch_shapes=[pltpu.VMEM(operand.shape, operand.dtype) for operand in operands]
        + [
            pltpu.VMEM((8, 2 * rim), F32),
            pltpu.VMEM((LANES, points), F32),
            pltpu.VMEM((points, LANES), F32),
            pltpu.VMEM((LANES, channels), BF),
            pltpu.VMEM((1, LANES), F32),
            pltpu.VMEM((2 * rim, 8), F32),
            pltpu.VMEM((owned + rim + LANES, channels), BF),
            pltpu.VMEM((2, rim, channels), BF),
            pltpu.VMEM((rim, channels), BF),
            pltpu.VMEM((edges, points, channels), F32),
            pltpu.VMEM((edges * largest, channels), F32),
            pltpu.VMEM((edges, points, channels), BF),
            wide_latents,
            pltpu.VMEM((points, LANES), F32),
            pltpu.VMEM((points, LANES), BF),
            pltpu.VMEM((n_member, share, LANES), BF),
            pltpu.VMEM((n_member, share, LANES), BF),
            pltpu.VMEM((points, LANES), BF),
            pltpu.VMEM((2, rim, channels), BF),
            pltpu.VMEM((2 * rim, channels), BF),
            dma((len(operands),)),
            dma((3,)),
            dma((3,)),
            dma,
            dma((len(PARTS),)),
            dma,
            dma((len(PARTS),)),
            dma((3,)),
            dma((3,)),
        ],
        compiler_params=pltpu.CompilerParams(
            collective_id=0, has_side_effects=True, vmem_limit_bytes=52 * 2**20
        ),
    )(*operands)
    d_grid, d_mesh = pl.pallas_call(
        finish,
        out_shape=(
            jax.ShapeDtypeStruct((points, channels), BF),
            jax.ShapeDtypeStruct((owned, channels), BF),
        ),
        in_specs=[vmem] * 3,
        out_specs=(anywhere, anywhere),
        scratch_shapes=[latents, dma((5,))],
        compiler_params=pltpu.CompilerParams(vmem_limit_bytes=16 * 2**20),
    )(d_grid, sums, w_src)
    return d_grid[None], d_mesh[None]


def solution(mesh):
    placed = (
        P("member", "band", None),
        P("member", "band", None),
        P(None, None, "band"),
        P("band", None),
        P("band", None),
        P(None, "band"),
        P(),
        P(),
        P(),
        P(),
        P(),
        P(),
        P(),
    )
    return jax.shard_map(
        functools.partial(per_device, mesh.shape["band"], mesh.shape["member"]),
        mesh=mesh,
        in_specs=placed,
        out_specs=(P("member", "band", None), P("member", "band", None)),
        check_vma=False,
    )
```
